256 devices in a mesh: tm: 32 (over y, z), head: 8 (over x, core).
Axes of the slice: x: 4, y: 4, z: 8, core: 2. Of those that a mesh axis runs over, the one named last changes fastest.
Arguments:
- query: bfloat16 [6144, 3072], P(('tm', 'head')), may hold values from -6 to 6
- keys: bfloat16 [6144, 3072], P(('tm', 'head')), may hold values from -6 to 6
- values: bfloat16 [6144, 3072], P(('tm', 'head')), may hold values from -6 to 6
- dout: bfloat16 [6144, 3072], P(('tm', 'head')), may hold values from -6 to 6
- slot_group: int32 [32], replicated, may hold values from 0 to 31, each once
- valid: int32 [32], replicated, may hold values from 48 to 192, as said below
Outputs:
- grad_query: bfloat16 [6144, 3072], P(('tm', 'head'))
- grad_keys: bfloat16 [6144, 3072], P(('tm', 'head'))
- grad_values: bfloat16 [6144, 3072], P(('tm', 'head'))
The draws below stay inside these ranges and needn't reach their ends.
Inputs may be any that keep to these rules, and one draw needn't show every extreme that they name: `slot_group`: each group number appears once. valid tokens are the first of each group; some group is full.
All inputs are finite; a program needn't handle non-finite values.
Results may differ from the reference program's by a relative error of at most 0.015.
Values may be sent and summed in bfloat16 or wider, within the bound.
No kernel may reach another device: no remote copies, remote signals or barrier semaphores. Data moves between devices by JAX's collectives and lax.ppermute only.
A program may use at most 64 MiB of HBM per device.

```python
import jax
import jax.numpy as jnp
from jax import lax

GROUP = 192
H = 24
HD = 128
GROUPS = 32
TOKENS = 6144


def draw_query(key, part):
    key = jax.random.fold_in(key, 11)
    field = jnp.clip(jax.random.normal(key, (TOKENS, H * HD), jnp.float32), -6.0, 6.0)
    return field.astype(jnp.bfloat16)


def draw_keys(key, part):
    key = jax.random.fold_in(key, 12)
    field = jnp.clip(jax.random.normal(key, (TOKENS, H * HD), jnp.float32), -6.0, 6.0)
    return field.astype(jnp.bfloat16)


def draw_valid(key, part):
    key = jax.random.fold_in(key, 13)
    first_key, second_key = jax.random.split(key)
    counts = jax.random.randint(first_key, (GROUPS,), GROUP // 4, GROUP + 1)
    filled = jax.random.randint(second_key, (), 0, GROUPS)
    counts = jnp.where(jnp.arange(GROUPS) == filled, GROUP, counts)
    return counts.astype(jnp.int32)


def block_levels(stream_key, extent, pieces, smallest, largest):
    gain = 1.0
    for position, blocks in pieces:
        heights = jax.random.uniform(jax.random.fold_in(jax.random.fold_in(stream_key, 6), position), (blocks,), jnp.float32, smallest / len(pieces), largest / len(pieces))
        gain = gain * jnp.repeat(jnp.exp(heights), extent[position] // blocks).reshape((-1,) + (1,) * (len(extent) - 1 - position))
    return gain


def bell_draw(key, shape, spread, reach, cuts=(), kind=jnp.bfloat16):
    result = spread * jax.random.normal(key, shape, jnp.float32)
    if cuts:
        result = result * block_levels(key, shape, cuts, -0.22, 0.18)
    return jnp.clip(result, -reach, reach).astype(kind)


def setup_inputs(seed: int = 0) -> dict:
    seeds = jax.random.split(jax.random.key(seed), 7)
    query = draw_query(jax.random.fold_in(seeds[6], 71), 0)
    keys = draw_keys(jax.random.fold_in(seeds[6], 71), 0)
    values = bell_draw(seeds[2], (TOKENS, H * HD), 1.0, 6.0, ((0, 256),))
    dout = bell_draw(seeds[3], (TOKENS, H * HD), 1.0, 6.0, ((0, 256),))
    slot_group = jax.random.permutation(seeds[4], GROUPS).astype(jnp.int32)
    valid = draw_valid(jax.random.fold_in(seeds[6], 71), 0)
    return {"query": query, "keys": keys, "values": values, "dout": dout, "slot_group": slot_group, "valid": valid}


NEG_FILL = -1e30


def reference(query, keys, values, dout, slot_group, valid):
    scale = 1.0 / (HD ** 0.5)
    positions = jnp.arange(TOKENS, dtype=jnp.int32)
    token_group = slot_group[positions // GROUP]
    token_live = (positions % GROUP) < valid[token_group]
    masked_dout = jnp.where(token_live[:, None], dout, jnp.zeros_like(dout))

    def split_heads(array):
        return array.reshape(TOKENS, H, HD).transpose(1, 0, 2)

    def merge_heads(array):
        return array.transpose(1, 0, 2).reshape(TOKENS, H * HD)

    def one_head(operands):
        head_query, head_keys, head_values, head_grad = operands

        def per_slot(carry, slot_index):
            key_grad, value_grad = carry
            first_row = (slot_index * GROUP).astype(jnp.int32)
            block_query = lax.dynamic_slice_in_dim(head_query, first_row, GROUP, 0)
            block_grad = lax.dynamic_slice_in_dim(head_grad, first_row, GROUP, 0)
            allowed = token_live & (token_group <= slot_group[slot_index])
            scores = jnp.dot(block_query, head_keys.T, preferred_element_type=jnp.float32) * scale
            scores = jnp.where(allowed[None, :], scores, NEG_FILL)
            row_max = jnp.max(scores, axis=1, keepdims=True)
            weights = jnp.where(allowed[None, :], jnp.exp(scores - row_max), 0.0)
            total = jnp.sum(weights, axis=1, keepdims=True)
            attended = jnp.dot(weights.astype(jnp.bfloat16), head_values, preferred_element_type=jnp.float32) / total
            log_total = row_max + jnp.log(total)
            delta = jnp.sum(block_grad.astype(jnp.float32) * attended, axis=1, keepdims=True)
            probs = jnp.where(allowed[None, :], jnp.exp(scores - log_total), 0.0)
            dprobs = jnp.dot(block_grad, head_values.T, preferred_element_type=jnp.float32)
            dscores = (probs * (dprobs - delta) * scale).astype(jnp.bfloat16)
            block_qgrad = jnp.dot(dscores, head_keys, preferred_element_type=jnp.float32)
            key_grad = key_grad + jnp.dot(dscores.T, block_query, preferred_element_type=jnp.float32)
            value_grad = value_grad + jnp.dot(probs.astype(jnp.bfloat16).T, block_grad, preferred_element_type=jnp.float32)
            return (key_grad, value_grad), block_qgrad.astype(jnp.bfloat16)

        start_carry = (jnp.zeros((TOKENS, HD), jnp.float32), jnp.zeros((TOKENS, HD), jnp.float32))
        (key_grad, value_grad), query_grad = lax.scan(per_slot, start_carry, jnp.arange(GROUPS, dtype=jnp.int32))
        return query_grad.reshape(TOKENS, HD), key_grad.astype(jnp.bfloat16), value_grad.astype(jnp.bfloat16)

    query_grad, key_grad, value_grad = lax.map(
        one_head, (split_heads(query), split_heads(keys), split_heads(values), split_heads(masked_dout)))
    return merge_heads(query_grad), merge_heads(key_grad), merge_heads(value_grad)
```

```python
import functools
import math

import jax
import jax.numpy as jnp
from jax import lax
from jax.experimental import pallas as pl
from jax.experimental.pallas import tpu as pltpu
from jax.sharding import PartitionSpec as P

HD = 128
HEADS = 3
COLS = HEADS * HD
NY, NZ, NX, NC = 4, 8, 4, 2
PART = 48
SUB = 24
GROUP = 192
QROWS = 768
NEG = -1e30
SCALE = 1.0 / math.sqrt(HD)
LOG2E = 1.4426950408889634
QCHUNK = 256

NT = (((1,), (1,)), ((), ()))
NN = (((1,), (0,)), ((), ()))
TN = (((0,), (0,)), ((), ()))


def pairs(move):
    out = []
    for y in range(NY):
        for z in range(NZ):
            for x in range(NX):
                for c in range(NC):
                    ty, tz, tx, tc = move(y, z, x, c)
                    ty, tz, tx = ty % NY, tz % NZ, tx % NX
                    out.append((((y * NZ + z) * NX + x) * NC + c, ((ty * NZ + tz) * NX + tx) * NC + tc))
    return out


def send(array, move):
    return lax.ppermute(array, ("tm", "head"), pairs(move))


def swap_core(array):
    return send(array, lambda y, z, x, c: (y, z, x, 1 - c))


def dot(a, b, dims):
    return lax.dot_general(a, b, dims, preferred_element_type=jnp.float32)


def row_positions(part):
    row = lax.broadcasted_iota(jnp.int32, (GROUP, QCHUNK), 0)
    piece = row // PART
    return PART * ((part - piece) & 3) + (row - PART * piece)


def pack_kernel(at, query, grad, keys, values, keep, give):
    z, c = at[1], at[3]
    for j in range(4):
        mine = pl.ds(pl.multiple_of(((z + c + 2 * j) & 7) * COLS, HD), COLS)
        theirs = pl.ds(pl.multiple_of(((z + 1 - c + 2 * j) & 7) * COLS, HD), COLS)
        for n, array in enumerate((query, grad, keys, values)):
            keep[j, n] = array[:, mine]
            give[j, n] = array[:, theirs]


def unpack_kernel(at, mine, theirs, *outs):
    z, c = at[1], at[3]
    for j in range(4):
        own = pl.ds(pl.multiple_of(((z + c + 2 * j) & 7) * COLS, HD), COLS)
        other = pl.ds(pl.multiple_of(((z + 1 - c + 2 * j) & 7) * COLS, HD), COLS)
        for n in range(3):
            outs[n][:, own] = mine[j, n]
            outs[n][:, other] = theirs[j, n]


def query_slot(at, s, j):
    return ((at[0] - s) & 3) * NZ + ((at[1] - at[3] - 2 * j) & 7)


def key_slot(at, ks):
    o = ks // 4
    core = at[3] + o - 2 * o * at[3]
    return at[0] * NZ + ((at[1] - core - 2 * (ks - 4 * o)) & 7)


def query_groups(at, groups):
    lane = lax.broadcasted_iota(jnp.int32, (1, QROWS), 1)
    out = jnp.zeros((1, QROWS), jnp.int32)
    for s in range(4):
        for j in range(4):
            out = jnp.where(lane >= (s * 4 + j) * PART, groups[query_slot(at, s, j)], out)
    return out


def stats_kernel(at, groups, valid, *refs):
    qd = refs[0:4]
    kv = refs[4:12]
    qbuf, kbuf, stats, pos_ref = refs[12:16]
    part = at[2]
    row = lax.broadcasted_iota(jnp.int32, (PART, COLS), 0) + part * PART
    for s in range(4):
        for j in range(4):
            rows = pl.ds((s * 4 + j) * PART, PART)
            live = row < valid[groups[query_slot(at, s, j)]]
            qbuf[0, rows, :] = qd[s][j, 0]
            grad = qd[s][j, 1]
            qbuf[1, rows, :] = jnp.where(live, grad, jnp.zeros_like(grad))
    for o in range(2):
        for s in range(4):
            for j in range(4):
                for a in range(2):
                    kbuf[a, o * 4 + j, pl.ds(s * PART, PART), :] = kv[o * 4 + s][j, a]
    pos_ref[...] = row_positions(part)
    qgrp = query_groups(at, groups)
    stats[...] = jnp.zeros_like(stats)
    for h in range(HEADS):
        cols = slice(h * HD, (h + 1) * HD)

        def step(ks, carry):
            key = kbuf[0, ks, :, cols]
            value = kbuf[1, ks, :, cols]
            group = groups[key_slot(at, ks)]
            live = pos_ref[...] < valid[group]
            out = []
            for n in range(QROWS // QCHUNK):
                rows = slice(n * QCHUNK, (n + 1) * QCHUNK)
                top, total, weighted = carry[n]
                scores = dot(key, qbuf[0, rows, cols], NT)
                dprobs = dot(value, qbuf[1, rows, cols], NT)
                scores = jnp.where(live, scores * (SCALE * LOG2E), NEG)
                ok = qgrp[:, rows] >= group
                new_top = jnp.where(ok, jnp.maximum(top, jnp.max(scores, axis=0, keepdims=True)), top)
                weights = jnp.exp2(scores - jnp.where(ok, new_top, -NEG))
                factor = jnp.exp2(top - new_top)
                total = total * factor + jnp.sum(weights, axis=0, keepdims=True)
                weighted = weighted * factor + jnp.sum(weights * dprobs, axis=0, keepdims=True)
                out.append((new_top, total, weighted))
            return tuple(out)

        start = (
            jnp.full((1, QCHUNK), NEG, jnp.float32),
            jnp.zeros((1, QCHUNK), jnp.float32),
            jnp.zeros((1, QCHUNK), jnp.float32),
        )
        final = lax.fori_loop(0, 8, step, (start,) * (QROWS // QCHUNK))
        for n in range(QROWS // QCHUNK):
            rows = slice(n * QCHUNK, (n + 1) * QCHUNK)
            stats[h : h + 1, rows] = final[n][0]
            stats[3 + h : 4 + h, rows] = final[n][1]
            stats[6 + h : 7 + h, rows] = final[n][2]


def grad_kernel(at, groups, valid, qbuf, kbuf, st0, st1, st2, st3, *refs):
    dq = refs[0:4]
    dkv = refs[4:12]
    pos_ref, log_ref, delta_ref, dqt = refs[12:16]
    pos_ref[...] = row_positions(at[2])
    qgrp = query_groups(at, groups)
    sts = [st0[...]]
    for shift, st in enumerate((st1, st2, st3), 1):
        moved = QROWS - shift * GROUP
        sts.append(jnp.concatenate([st[:, moved:], st[:, :moved]], axis=1))
    tops = [st[0:3, :] for st in sts]
    top = functools.reduce(jnp.maximum, tops)
    factors = [jnp.exp2(t - top) for t in tops]
    total = sum(f * st[3:6, :] for f, st in zip(factors, sts))
    weighted = sum(f * st[6:9, :] for f, st in zip(factors, sts))
    log_ref[0:3, :] = top + jnp.log2(total)
    delta_ref[0:3, :] = weighted / total
    dqt[...] = jnp.zeros_like(dqt)
    for h in range(HEADS):
        cols = slice(h * HD, (h + 1) * HD)
        for o in range(2):

            def step(j, _):
                ks = o * 4 + j
                key = kbuf[0, ks, :, cols]
                value = kbuf[1, ks, :, cols]
                group = groups[key_slot(at, ks)]
                live = pos_ref[...] < valid[group]
                key_grad = jnp.zeros((GROUP, HD), jnp.float32)
                value_grad = jnp.zeros((GROUP, HD), jnp.float32)
                for n in range(QROWS // QCHUNK):
                    rows = slice(n * QCHUNK, (n + 1) * QCHUNK)
                    query = qbuf[0, rows, cols]
                    grad = qbuf[1, rows, cols]
                    scores = dot(key, query, NT)
                    dprobs = dot(value, grad, NT)
                    level = jnp.where(qgrp[:, rows] >= group, log_ref[h : h + 1, rows], -NEG)
                    probs = jnp.exp2(jnp.where(live, scores * (SCALE * LOG2E), NEG) - level)
                    dscores = (probs * (dprobs - delta_ref[h : h + 1, rows])).astype(jnp.bfloat16)
                    value_grad += dot(probs.astype(jnp.bfloat16), grad, NN)
                    key_grad += dot(dscores, query, NN)
                    dqt[h, :, rows] += dot(key, dscores, TN)
                key_grad = (key_grad * SCALE).astype(jnp.bfloat16)
                value_grad = value_grad.astype(jnp.bfloat16)
                for s in range(4):
                    piece = slice(s * PART, (s + 1) * PART)
                    dkv[o * 4 + s][j, 0, :, cols] = key_grad[piece]
                    dkv[o * 4 + s][j, 1, :, cols] = value_grad[piece]
                return 0

            lax.fori_loop(0, 4, step, 0)
        query_grad = (dqt[h] * SCALE).T.astype(jnp.bfloat16)
        for s in range(4):
            for j in range(4):
                first = (s * 4 + j) * PART
                dq[s][j, :, cols] = query_grad[first : first + PART]


SMEM = pl.BlockSpec(memory_space=pltpu.SMEM)
VMEM = pl.BlockSpec(memory_space=pltpu.VMEM)
PARAMS = pltpu.CompilerParams(vmem_limit_bytes=48 * 1024 * 1024)


def local(query, keys, values, dout, slot_group, valid):
    tm = lax.axis_index("tm")
    head = lax.axis_index("head")
    y, z, x, c = tm // NZ, tm % NZ, head // NC, head % NC
    at = jnp.stack([y, z, x, c])
    bf16, f32 = jnp.bfloat16, jnp.float32

    keep, give = pl.pallas_call(
        pack_kernel,
        out_shape=(jax.ShapeDtypeStruct((4, 4, SUB, COLS), bf16),) * 2,
        in_specs=[SMEM] + [VMEM] * 4,
        out_specs=(VMEM,) * 2,
        name="pack",
    )(at, query, dout, keys, values)
    take = swap_core(give)
    both = jnp.where(c == 0, jnp.concatenate([keep, take], axis=2), jnp.concatenate([take, keep], axis=2))
    received = [send(both[j], lambda y, z, x, c: (y, z + c + 2 * j, x, c)) for j in range(4)]
    own_qd = jnp.stack([r[0:2] for r in received])
    own_kv = jnp.stack([r[2:4] for r in received])

    kvs = [own_kv] + [send(own_kv, lambda y, z, x, c: (y, z, x + s, c)) for s in (1, 2, 3)]
    qds = [own_qd] + [send(own_qd, lambda y, z, x, c: (y + s, z, x, c)) for s in (1, 2, 3)]
    kvs = kvs + [swap_core(kv) for kv in kvs]

    qbuf, kbuf, stats = pl.pallas_call(
        stats_kernel,
        out_shape=(
            jax.ShapeDtypeStruct((2, QROWS, COLS), bf16),
            jax.ShapeDtypeStruct((2, 8, GROUP, COLS), bf16),
            jax.ShapeDtypeStruct((16, QROWS), f32),
        ),
        in_specs=[SMEM] * 3 + [VMEM] * 12,
        out_specs=(VMEM,) * 3,
        scratch_shapes=[pltpu.VMEM((GROUP, QCHUNK), jnp.int32)],
        compiler_params=PARAMS,
        name="stats",
    )(at, slot_group, valid, *qds, *kvs)

    all_stats = [stats] + [send(stats, lambda y, z, x, c: (y + s, z, x, c)) for s in (1, 2, 3)]

    outs = pl.pallas_call(
        grad_kernel,
        out_shape=(jax.ShapeDtypeStruct((4, PART, COLS), bf16),) * 4
        + (jax.ShapeDtypeStruct((4, 2, PART, COLS), bf16),) * 8,
        in_specs=[SMEM] * 3 + [VMEM] * 6,
        out_specs=(VMEM,) * 12,
        scratch_shapes=[
            pltpu.VMEM((GROUP, QCHUNK), jnp.int32),
            pltpu.VMEM((8, QROWS), f32),
            pltpu.VMEM((8, QROWS), f32),
            pltpu.VMEM((HEADS, HD, QROWS), f32),
        ],
        compiler_params=PARAMS,
        name="grads",
    )(at, slot_group, valid, qbuf, kbuf, *all_stats)
    dq, dkv_own, dkv_other = outs[0:4], outs[4:8], outs[8:12]

    dq_got = [send(dq[s], lambda y, z, x, c: (y - s, z, x, c)) for s in (1, 2, 3)]
    dkv = [a.astype(f32) + swap_core(b).astype(f32) for a, b in zip(dkv_own, dkv_other)]
    dkv_got = [send(dkv[s].astype(bf16), lambda y, z, x, c: (y, z, x - s, c)) for s in (1, 2, 3)]
    dq_sum = (dq[0].astype(f32) + sum(g.astype(f32) for g in dq_got)).astype(bf16)
    dkv_sum = (dkv[0] + sum(g.astype(f32) for g in dkv_got)).astype(bf16)

    back = []
    for j in range(4):
        block = jnp.concatenate([dq_sum[j][None], dkv_sum[j]], axis=0)
        back.append(send(block, lambda y, z, x, c: (y, z - c - 2 * j, x, c)))
    first = jnp.stack([b[:, :SUB] for b in back])
    second = jnp.stack([b[:, SUB:] for b in back])
    theirs = swap_core(jnp.where(c == 0, second, first))
    return pl.pallas_call(
        unpack_kernel,
        out_shape=(jax.ShapeDtypeStruct((SUB, NZ * COLS), bf16),) * 3,
        in_specs=[SMEM] + [VMEM] * 2,
        out_specs=(VMEM,) * 3,
        name="unpack",
    )(at, jnp.where(c == 0, first, second), theirs)


def solution(mesh):
    spec = P(("tm", "head"), None)
    return jax.shard_map(
        local,
        mesh=mesh,
        in_specs=(spec, spec, spec, spec, P(), P()),
        out_specs=(spec, spec, spec),
        check_vma=False,
    )
```

```python
import functools
import math

import jax
import jax.numpy as jnp
from jax import lax
from jax.experimental import pallas as pl
from jax.experimental.pallas import tpu as pltpu
from jax.sharding import PartitionSpec as P

HD = 128
HEADS = 3
COLS = HEADS * HD
NY, NZ, NX, NC = 4, 8, 4, 2
PART = 48
SUB = 24
QROWS = 768
NEG = -1e30
LOW = -1e29
FAR = 1000
SCALE = 1.0 / math.sqrt(HD)
LOG2E = 1.4426950408889634
QCHUNK = 256
KROWS = 1536
KCHUNK = 256

NT = (((1,), (1,)), ((), ()))
NN = (((1,), (0,)), ((), ()))
TN = (((0,), (0,)), ((), ()))


def pairs(move):
    out = []
    for y in range(NY):
        for z in range(NZ):
            for x in range(NX):
                for c in range(NC):
                    ty, tz, tx, tc = move(y, z, x, c)
                    ty, tz, tx = ty % NY, tz % NZ, tx % NX
                    out.append((((y * NZ + z) * NX + x) * NC + c, ((ty * NZ + tz) * NX + tx) * NC + tc))
    return out


def send(array, move):
    return lax.ppermute(array, ("tm", "head"), pairs(move))


def swap_core(array):
    return send(array, lambda y, z, x, c: (y, z, x, 1 - c))


def dot(a, b, dims):
    return lax.dot_general(a, b, dims, preferred_element_type=jnp.float32)


def pack_kernel(at, query, grad, keys, values, keep, give):
    z, c = at[1], at[3]
    for j in range(4):
        mine = pl.ds(pl.multiple_of(((z + c + 2 * j) & 7) * COLS, HD), COLS)
        theirs = pl.ds(pl.multiple_of(((z + 1 - c + 2 * j) & 7) * COLS, HD), COLS)
        for n, array in enumerate((query, grad, keys, values)):
            keep[j, n] = array[:, mine]
            give[j, n] = array[:, theirs]


def unpack_kernel(at, mine, theirs, *outs):
    z, c = at[1], at[3]
    for j in range(4):
        own = pl.ds(pl.multiple_of(((z + c + 2 * j) & 7) * COLS, HD), COLS)
        other = pl.ds(pl.multiple_of(((z + 1 - c + 2 * j) & 7) * COLS, HD), COLS)
        for n in range(3):
            outs[n][:, own] = mine[j, n]
            outs[n][:, other] = theirs[j, n]


def flip(s, core):
    return (0, 1 + 2 * core, 3 - 2 * core, 2)[s]


def query_slot(at, s, j):
    return (at[0] ^ flip(s, at[3])) * NZ + ((at[1] - at[3] - 2 * j) & 7)


def key_slot(at, o, j):
    core = 1 - at[3] if o else at[3]
    return at[0] * NZ + ((at[1] - core - 2 * j) & 7)


def key_part(at, o, s):
    return at[2] ^ flip(s, 1 - at[3] if o else at[3])


def first_y(array):
    return send(array, lambda y, z, x, c: (y ^ (1 + 2 * c), z, x, c))


def second_y(array):
    return send(array, lambda y, z, x, c: (y ^ (3 - 2 * c), z, x, c))


def first_x(array):
    return send(array, lambda y, z, x, c: (y, z, x ^ (1 + 2 * c), c))


def second_x(array):
    return send(array, lambda y, z, x, c: (y, z, x ^ (3 - 2 * c), c))


def pieces(own, first, rest):
    return (own, first, rest.at[0], rest.at[1])


def clip_rows(count):
    return jnp.minimum(jnp.maximum(count, 0), PART)


def round_rows(count):
    return ((count + 15) // 16) * 16


def place(at, groups, valid):
    part = at[2]
    slots = [(s, j) for s in range(4) for j in range(4)]
    q_group = [groups[query_slot(at, s, j)] for s, j in slots]
    q_live = [clip_rows(valid[g] - PART * part) for g in q_group]
    q_first = [
        sum(jnp.where(other < mine, round_rows(live), 0) for other, live in zip(q_group, q_live))
        for mine in q_group
    ]
    k_group = [groups[key_slot(at, o, j)] for o in range(2) for j in range(4)]
    k_valid = [valid[g] for g in k_group]
    k_first, k_live = [], []
    for ks, (mine, count) in enumerate(zip(k_group, k_valid)):
        first = sum(jnp.where(other < mine, round_rows(n), 0) for other, n in zip(k_group, k_valid))
        firsts, lives = [], []
        for s in range(4):
            live = clip_rows(count - PART * key_part(at, ks // 4, s))
            firsts.append(first)
            lives.append(live)
            first = first + round_rows(live)
        k_first.append(firsts)
        k_live.append(lives)
    q_total = sum(round_rows(live) for live in q_live)
    blocks = []
    for n in range(QROWS // QCHUNK):
        top = functools.reduce(
            jnp.maximum,
            [
                jnp.where((first < QCHUNK * (n + 1)) & (live > 0), g, -1)
                for g, first, live in zip(q_group, q_first, q_live)
            ],
        )
        rows = sum(jnp.where(g <= top, round_rows(v), 0) for g, v in zip(k_group, k_valid))
        blocks.append(jnp.where(q_total > QCHUNK * n, (rows + KCHUNK - 1) // KCHUNK, 0))
    return q_group, q_live, q_first, k_group, k_live, k_first, blocks


def aligned(first):
    return pl.ds(pl.multiple_of(first, 16), PART)


def stats_kernel(at, groups, valid, *refs):
    qd = pieces(*refs[0:3])
    kv = pieces(*refs[3:6]) + pieces(*refs[6:9])
    qbuf, kbuf, kgrp, qgrp, stats = refs[9:14]
    q_group, q_live, q_first, k_group, k_live, k_first, blocks = place(at, groups, valid)
    qbuf[...] = jnp.zeros_like(qbuf)
    kbuf[...] = jnp.zeros_like(kbuf)
    kgrp[...] = jnp.full_like(kgrp, FAR)
    row = lax.broadcasted_iota(jnp.int32, (PART, COLS), 0)
    row_lanes = lax.broadcasted_iota(jnp.int32, (PART, HD), 0)
    lane = lax.broadcasted_iota(jnp.int32, (8, QROWS), 1)
    lane_group = jnp.full((8, QROWS), -1, jnp.int32)
    for s in range(4):
        for j in range(4):
            n = s * 4 + j
            rows = aligned(q_first[n])
            live = row < q_live[n]
            for a in range(2):
                qbuf[a, rows, :] = jnp.where(live, qd[s][j, a], qbuf[a, rows, :])
            here = (lane >= q_first[n]) & (lane < q_first[n] + q_live[n])
            lane_group = jnp.where(here, q_group[n], lane_group)
    qgrp[...] = lane_group
    for o in range(2):
        for j in range(4):
            ks = o * 4 + j
            for s in range(4):
                rows = aligned(k_first[ks][s])
                live = row < k_live[ks][s]
                for a in range(2):
                    kbuf[a, rows, :] = jnp.where(live, kv[o * 4 + s][j, a], kbuf[a, rows, :])
                kgrp[rows, :] = jnp.where(row_lanes < k_live[ks][s], k_group[ks], kgrp[rows, :])
    stats[...] = jnp.zeros_like(stats)
    for n in range(QROWS // QCHUNK):
        rows = slice(n * QCHUNK, (n + 1) * QCHUNK)

        def step(kb, carry):
            keys = pl.ds(pl.multiple_of(kb * KCHUNK, KCHUNK), KCHUNK)
            group = kgrp[keys, :]
            ok = jnp.concatenate([group] * (QCHUNK // HD), axis=1) <= qgrp[0:1, rows]
            out = []
            for h in range(HEADS):
                cols = slice(h * HD, (h + 1) * HD)
                top, total, weighted = carry[h]
                scores = dot(kbuf[0, keys, cols], qbuf[0, rows, cols], NT)
                dprobs = dot(kbuf[1, keys, cols], qbuf[1, rows, cols], NT)
                scores = jnp.where(ok, scores * (SCALE * LOG2E), NEG)
                new_top = jnp.maximum(top, jnp.max(scores, axis=0, keepdims=True))
                weights = jnp.exp2(scores - new_top)
                factor = jnp.exp2(top - new_top)
                total = total * factor + jnp.sum(weights, axis=0, keepdims=True)
                weighted = weighted * factor + jnp.sum(weights * dprobs, axis=0, keepdims=True)
                out.append((new_top, total, weighted))
            return tuple(out)

        start = (
            jnp.full((1, QCHUNK), LOW, jnp.float32),
            jnp.zeros((1, QCHUNK), jnp.float32),
            jnp.zeros((1, QCHUNK), jnp.float32),
        )
        final = lax.fori_loop(0, blocks[n], step, (start,) * HEADS)
        for h in range(HEADS):
            for k in range(3):
                stats[3 * k + h : 3 * k + h + 1, rows] = final[h][k]


def grad_kernel(at, groups, valid, qbuf, kbuf, kgrp, qgrp, st0, st1, st23, *refs):
    dq, *dkv = refs[0:3]
    log_ref, delta_ref, dqt, dqs, dks, dvs = refs[3:9]
    q_group, q_live, q_first, k_group, k_live, k_first, blocks = place(at, groups, valid)
    sts = [st0[...], st1[...], st23[0], st23[1]]
    top = functools.reduce(jnp.maximum, [st[0:3, :] for st in sts])
    factors = [jnp.exp2(st[0:3, :] - top) for st in sts]
    total = sum(f * st[3:6, :] for f, st in zip(factors, sts))
    weighted = sum(f * st[6:9, :] for f, st in zip(factors, sts))
    some = total > 0.0
    safe = jnp.where(some, total, 1.0)
    log_ref[0:3, :] = jnp.where(some, top + jnp.log2(safe), 0.0)
    delta_ref[0:3, :] = weighted / safe
    dqt[...] = jnp.zeros_like(dqt)
    dks[...] = jnp.zeros_like(dks)
    dvs[...] = jnp.zeros_like(dvs)
    for n in range(QROWS // QCHUNK):
        rows = slice(n * QCHUNK, (n + 1) * QCHUNK)

        def step(kb, _):
            keys = pl.ds(pl.multiple_of(kb * KCHUNK, KCHUNK), KCHUNK)
            group = kgrp[keys, :]
            ok = jnp.concatenate([group] * (QCHUNK // HD), axis=1) <= qgrp[0:1, rows]
            for h in range(HEADS):
                cols = slice(h * HD, (h + 1) * HD)
                key = kbuf[0, keys, cols]
                query = qbuf[0, rows, cols]
                grad = qbuf[1, rows, cols]
                scores = dot(key, query, NT)
                dprobs = dot(kbuf[1, keys, cols], grad, NT)
                scores = jnp.where(ok, scores * (SCALE * LOG2E), NEG)
                probs = jnp.exp2(scores - log_ref[h : h + 1, rows])
                dscores = (probs * (dprobs - delta_ref[h : h + 1, rows])).astype(jnp.bfloat16)
                dvs[keys, cols] += dot(probs.astype(jnp.bfloat16), grad, NN)
                dks[keys, cols] += dot(dscores, query, NN)
                dqt[h, :, rows] += dot(key, dscores, TN)
            return 0

        lax.fori_loop(0, blocks[n], step, 0)
    for h in range(HEADS):
        dqs[:, h * HD : (h + 1) * HD] = (dqt[h] * SCALE).T
    row = lax.broadcasted_iota(jnp.int32, (PART, COLS), 0)
    for o in range(2):
        for j in range(4):
            ks = o * 4 + j
            for s in range(4):
                rows = aligned(k_first[ks][s])
                live = row < k_live[ks][s]
                dkv[o][s, j, 0] = jnp.where(live, dks[rows, :] * SCALE, 0.0).astype(jnp.bfloat16)
                dkv[o][s, j, 1] = jnp.where(live, dvs[rows, :], 0.0).astype(jnp.bfloat16)
    for s in range(4):
        for j in range(4):
            n = s * 4 + j
            dq[s, j] = jnp.where(row < q_live[n], dqs[aligned(q_first[n]), :], 0.0).astype(jnp.bfloat16)


SMEM = pl.BlockSpec(memory_space=pltpu.SMEM)
VMEM = pl.BlockSpec(memory_space=pltpu.VMEM)
PARAMS = pltpu.CompilerParams(vmem_limit_bytes=48 * 1024 * 1024)


def local(query, keys, values, dout, slot_group, valid):
    tm = lax.axis_index("tm")
    head = lax.axis_index("head")
    y, z, x, c = tm // NZ, tm % NZ, head // NC, head % NC
    at = jnp.stack([y, z, x, c])
    bf16, f32 = jnp.bfloat16, jnp.float32

    keep, give = pl.pallas_call(
        pack_kernel,
        out_shape=(jax.ShapeDtypeStruct((4, 4, SUB, COLS), bf16),) * 2,
        in_specs=[SMEM] + [VMEM] * 4,
        out_specs=(VMEM,) * 2,
        name="pack",
    )(at, query, dout, keys, values)
    take = swap_core(give)
    both = jnp.where(c == 0, jnp.concatenate([keep, take], axis=2), jnp.concatenate([take, keep], axis=2))
    received = {j: send(both[j], lambda y, z, x, c: (y, z + c + 2 * j, x, c)) for j in (2, 1, 3, 0)}
    ordered = [received[j] for j in range(4)]
    own_qd = jnp.stack([r[0:2] for r in ordered])
    own_kv = jnp.stack([r[2:4] for r in ordered])

    kv_first = first_x(own_kv)
    qd_first = first_y(own_qd)
    kv_first, qd_first = lax.optimization_barrier((kv_first, qd_first))
    kv_rest = second_x(jnp.stack([own_kv, kv_first]))
    qd_rest = second_y(jnp.stack([own_qd, qd_first]))
    kvs = [own_kv, kv_first, kv_rest]
    kvs = kvs + [swap_core(kv) for kv in kvs]
    qds = [own_qd, qd_first, qd_rest]

    i32 = jnp.int32
    qbuf, kbuf, kgrp, qgrp, stats = pl.pallas_call(
        stats_kernel,
        out_shape=(
            jax.ShapeDtypeStruct((2, QROWS, COLS), bf16),
            jax.ShapeDtypeStruct((2, KROWS, COLS), bf16),
            jax.ShapeDtypeStruct((KROWS, HD), i32),
            jax.ShapeDtypeStruct((8, QROWS), i32),
            jax.ShapeDtypeStruct((16, QROWS), f32),
        ),
        in_specs=[SMEM] * 3 + [VMEM] * 9,
        out_specs=(VMEM,) * 5,
        compiler_params=PARAMS,
        name="stats",
    )(at, slot_group, valid, *qds, *kvs)

    stats_first = first_y(stats)
    stats_rest = second_y(jnp.stack([stats, stats_first]))

    dq, dkv_own, dkv_other = pl.pallas_call(
        grad_kernel,
        out_shape=(jax.ShapeDtypeStruct((4, 4, PART, COLS), bf16),)
        + (jax.ShapeDtypeStruct((4, 4, 2, PART, COLS), bf16),) * 2,
        in_specs=[SMEM] * 3 + [VMEM] * 7,
        out_specs=(VMEM,) * 3,
        scratch_shapes=[
            pltpu.VMEM((8, QROWS), f32),
            pltpu.VMEM((8, QROWS), f32),
            pltpu.VMEM((HEADS, HD, QROWS), f32),
            pltpu.VMEM((QROWS, COLS), f32),
            pltpu.VMEM((KROWS, COLS), f32),
            pltpu.VMEM((KROWS, COLS), f32),
        ],
        compiler_params=PARAMS,
        name="grads",
    )(at, slot_group, valid, qbuf, kbuf, kgrp, qgrp, stats, stats_first, stats_rest)

    swapped, dq_half = lax.optimization_barrier((swap_core(dkv_other), second_y(dq[2:4])))
    dkv_sum = dkv_own.astype(f32) + swapped.astype(f32)
    dq_sum = dq[0:2].astype(f32) + dq_half.astype(f32)
    dkv_half, dq_last = lax.optimization_barrier(
        (second_x(dkv_sum[2:4].astype(bf16)), first_y(dq_sum[1].astype(bf16)))
    )
    dkv_sum = dkv_sum[0:2] + dkv_half.astype(f32)
    dkv_last = first_x(dkv_sum[1].astype(bf16))
    dkv_sum = (dkv_sum[0] + dkv_last.astype(f32)).astype(bf16)
    dq_sum = (dq_sum[0] + dq_last.astype(f32)).astype(bf16)

    back = {}
    for j in (2, 1, 3, 0):
        block = jnp.concatenate([dq_sum[j][None], dkv_sum[j]], axis=0)
        back[j] = send(block, lambda y, z, x, c: (y, z - c - 2 * j, x, c))
    back = [back[j] for j in range(4)]
    first = jnp.stack([b[:, :SUB] for b in back])
    second = jnp.stack([b[:, SUB:] for b in back])
    theirs = swap_core(jnp.where(c == 0, second, first))
    return pl.pallas_call(
        unpack_kernel,
        out_shape=(jax.ShapeDtypeStruct((SUB, NZ * COLS), bf16),) * 3,
        in_specs=[SMEM] + [VMEM] * 2,
        out_specs=(VMEM,) * 3,
        name="unpack",
    )(at, jnp.where(c == 0, first, second), theirs)


def solution(mesh):
    spec = P(("tm", "head"), None)
    return jax.shard_map(
        local,
        mesh=mesh,
        in_specs=(spec, spec, spec, spec, P(), P()),
        out_specs=(spec, spec, spec),
        check_vma=False,
    )
```

```python
import functools
import math

import jax
import jax.numpy as jnp
from jax import lax
from jax.experimental import pallas as pl
from jax.experimental.pallas import tpu as pltpu
from jax.sharding import PartitionSpec as P

HD = 128
HEADS = 3
COLS = HEADS * HD
NY, NZ, NX, NC = 4, 8, 4, 2
PART = 48
SUB = 24
QROWS = 768
NEG = -1e30
LOW = -1e29
FAR = 1000
SCALE = 1.0 / math.sqrt(HD)
LOG2E = 1.4426950408889634
QCHUNK = 256
KROWS = 768
KCHUNK = 512

NT = (((1,), (1,)), ((), ()))
NN = (((1,), (0,)), ((), ()))
TN = (((0,), (0,)), ((), ()))


def pairs(move):
    out = []
    for y in range(NY):
        for z in range(NZ):
            for x in range(NX):
                for c in range(NC):
                    ty, tz, tx, tc = move(y, z, x, c)
                    ty, tz, tx = ty % NY, tz % NZ, tx % NX
                    out.append((((y * NZ + z) * NX + x) * NC + c, ((ty * NZ + tz) * NX + tx) * NC + tc))
    return out


def send(array, move):
    return lax.ppermute(array, ("tm", "head"), pairs(move))


def swap_core(array):
    return send(array, lambda y, z, x, c: (y, z, x, 1 - c))


def dot(a, b, dims):
    return lax.dot_general(a, b, dims, preferred_element_type=jnp.float32)


def position():
    tm = lax.axis_index("tm")
    head = lax.axis_index("head")
    return tm // NZ, tm % NZ, head // NC, head % NC


def pack_kernel(query, grad, keys, values, keep, give):
    _, z, _, c = position()
    for j in range(4):
        mine = pl.ds(pl.multiple_of(((z + c + 2 * j) & 7) * COLS, HD), COLS)
        theirs = pl.ds(pl.multiple_of(((z + 1 - c + 2 * j) & 7) * COLS, HD), COLS)
        for n, array in enumerate((query, grad, keys, values)):
            keep[j, n] = array[:, mine]
            give[j, n] = array[:, theirs]


def unpack_kernel(mine, theirs, *outs):
    _, z, _, c = position()
    for j in range(4):
        own = pl.ds(pl.multiple_of(((z + c + 2 * j) & 7) * COLS, HD), COLS)
        other = pl.ds(pl.multiple_of(((z + 1 - c + 2 * j) & 7) * COLS, HD), COLS)
        for n in range(3):
            outs[n][:, own] = mine[j, n]
            outs[n][:, other] = theirs[j, n]


def flip(s, core):
    return (0, 1 + 2 * core, 3 - 2 * core, 2)[s]


def query_slot(at, s, j):
    return (at[0] ^ flip(s, at[3])) * NZ + ((at[1] - at[3] - 2 * j) & 7)


def key_slot(at, o, j):
    core = 1 - at[3] if o else at[3]
    return at[0] * NZ + ((at[1] - core - 2 * j) & 7)


def key_part(at, o, s):
    return at[2] ^ flip(s, 1 - at[3] if o else at[3])


def first_y(array):
    return send(array, lambda y, z, x, c: (y ^ (1 + 2 * c), z, x, c))


def second_y(array):
    return send(array, lambda y, z, x, c: (y ^ (3 - 2 * c), z, x, c))


def first_x(array):
    return send(array, lambda y, z, x, c: (y, z, x ^ (1 + 2 * c), c))


def second_x(array):
    return send(array, lambda y, z, x, c: (y, z, x ^ (3 - 2 * c), c))


def pieces(own, first, rest):
    return (own, first, rest.at[0], rest.at[1])


def clip_rows(count):
    return jnp.minimum(jnp.maximum(count, 0), PART)


def round_rows(count):
    return ((count + 15) // 16) * 16


def place_queries(at, groups, valid):
    group = [groups[query_slot(at, s, j)] for s in range(4) for j in range(4)]
    live = [clip_rows(valid[g] - PART * at[2]) for g in group]
    padded = [round_rows(n) for n in live]
    first = [sum(jnp.where(other < mine, n, 0) for other, n in zip(group, padded)) for mine in group]
    tops = []
    for n in range(QROWS // QCHUNK):
        inside = [
            jnp.where((f < QCHUNK * (n + 1)) & (count > 0), g, -1) for g, f, count in zip(group, first, live)
        ]
        tops.append(jnp.where(sum(padded) > QCHUNK * n, functools.reduce(jnp.maximum, inside), -1))
    return group, live, first, tops


def place_keys(at, groups, valid, o, tops):
    group = [groups[key_slot(at, o, j)] for j in range(4)]
    rows = [round_rows(valid[g]) for g in group]
    first, live = [], []
    for mine in group:
        here = sum(jnp.where(other < mine, n, 0) for other, n in zip(group, rows))
        firsts, lives = [], []
        for s in range(4):
            count = clip_rows(valid[mine] - PART * key_part(at, o, s))
            firsts.append(here)
            lives.append(count)
            here = here + round_rows(count)
        first.append(firsts)
        live.append(lives)
    half = KCHUNK // 2
    blocks = []
    for top in tops:
        seen = sum(jnp.where(g <= top, n, 0) for g, n in zip(group, rows))
        blocks.append((seen + half - 1) // half)
    return group, live, first, blocks


def visit(blocks, step, state):
    half = KCHUNK // 2
    whole = blocks // 2
    state = lax.fori_loop(0, whole, lambda i, v: step(pl.ds(pl.multiple_of(i * KCHUNK, KCHUNK), KCHUNK), v), state)
    return lax.fori_loop(
        0, blocks - 2 * whole, lambda i, v: step(pl.ds(pl.multiple_of(whole * KCHUNK, KCHUNK), half), v), state
    )


def aligned(first):
    return pl.ds(pl.multiple_of(first, 16), PART)


def load_queries(qd, qbuf, qgrp, q_group, q_live, q_first):
    qbuf[...] = jnp.zeros_like(qbuf)
    row = lax.broadcasted_iota(jnp.int32, (PART, COLS), 0)
    lane = lax.broadcasted_iota(jnp.int32, (8, QROWS), 1)
    lane_group = jnp.full((8, QROWS), -1, jnp.int32)
    for s in range(4):
        for j in range(4):
            n = s * 4 + j
            rows = aligned(q_first[n])
            live = row < q_live[n]
            for a in range(2):
                qbuf[a, rows, :] = jnp.where(live, qd[s][j, a], qbuf[a, rows, :])
            here = (lane >= q_first[n]) & (lane < q_first[n] + q_live[n])
            lane_group = jnp.where(here, q_group[n], lane_group)
    qgrp[...] = lane_group


def load_keys(kv, kbuf, kgrp, k_group, k_live, k_first):
    kbuf[...] = jnp.zeros_like(kbuf)
    kgrp[...] = jnp.full_like(kgrp, FAR)
    row = lax.broadcasted_iota(jnp.int32, (PART, COLS), 0)
    row_lanes = lax.broadcasted_iota(jnp.int32, (PART, HD), 0)
    for j in range(4):
        for s in range(4):
            rows = aligned(k_first[j][s])
            live = row < k_live[j][s]
            for a in range(2):
                kbuf[a, rows, :] = jnp.where(live, kv[s][j, a], kbuf[a, rows, :])
            kgrp[rows, :] = jnp.where(row_lanes < k_live[j][s], k_group[j], kgrp[rows, :])


def stats_kernel(o, groups, valid, *refs):
    at = position()
    q_group, q_live, q_first, tops = place_queries(at, groups, valid)
    k_group, k_live, k_first, blocks = place_keys(at, groups, valid, o, tops)
    if o == 0:
        qbuf, qgrp, kbuf, kgrp, stats = refs[6:11]
        load_queries(pieces(*refs[0:3]), qbuf, qgrp, q_group, q_live, q_first)
    else:
        qbuf, qgrp, before = refs[0:3]
        kbuf, kgrp, stats = refs[6:9]
    load_keys(pieces(*refs[3:6]), kbuf, kgrp, k_group, k_live, k_first)
    stats[...] = jnp.zeros_like(stats)
    for n in range(QROWS // QCHUNK):
        rows = slice(n * QCHUNK, (n + 1) * QCHUNK)

        def step(keys, carry):
            group = kgrp[keys, :]
            ok = jnp.concatenate([group] * (QCHUNK // HD), axis=1) <= qgrp[0:1, rows]
            out = []
            for h in range(HEADS):
                cols = slice(h * HD, (h + 1) * HD)
                top, total, weighted = carry[h]
                scores = dot(kbuf[0, keys, cols], qbuf[0, rows, cols], NT)
                dprobs = dot(kbuf[1, keys, cols], qbuf[1, rows, cols], NT)
                scores = jnp.where(ok, scores * (SCALE * LOG2E), NEG)
                new_top = jnp.maximum(top, jnp.max(scores, axis=0, keepdims=True))
                weights = jnp.exp2(scores - new_top)
                factor = jnp.exp2(top - new_top)
                total = total * factor + jnp.sum(weights, axis=0, keepdims=True)
                weighted = weighted * factor + jnp.sum(weights * dprobs, axis=0, keepdims=True)
                out.append((new_top, total, weighted))
            return tuple(out)

        if o == 0:
            start = (
                jnp.full((1, QCHUNK), LOW, jnp.float32),
                jnp.zeros((1, QCHUNK), jnp.float32),
                jnp.zeros((1, QCHUNK), jnp.float32),
            )
            start = (start,) * HEADS
        else:
            start = tuple(
                tuple(before[3 * k + h : 3 * k + h + 1, rows] for k in range(3)) for h in range(HEADS)
            )
        final = visit(blocks[n], step, start)
        for h in range(HEADS):
            for k in range(3):
                stats[3 * k + h : 3 * k + h + 1, rows] = final[h][k]


def combine(st0, st1, st23, levels):
    sts = [st0[...], st1[...], st23[0], st23[1]]
    top = functools.reduce(jnp.maximum, [st[0:3, :] for st in sts])
    factors = [jnp.exp2(st[0:3, :] - top) for st in sts]
    total = sum(f * st[3:6, :] for f, st in zip(factors, sts))
    weighted = sum(f * st[6:9, :] for f, st in zip(factors, sts))
    some = total > 0.0
    safe = jnp.where(some, total, 1.0)
    levels[0:3, :] = jnp.where(some, top + jnp.log2(safe), 0.0)
    levels[3:6, :] = weighted / safe
    levels[6:8, :] = jnp.zeros_like(levels[6:8, :])


def grad_kernel(o, groups, valid, qbuf, qgrp, kbuf, kgrp, *refs):
    at = position()
    q_group, q_live, q_first, tops = place_queries(at, groups, valid)
    k_group, k_live, k_first, blocks = place_keys(at, groups, valid, o, tops)
    if o == 1:
        dkv, dqt, levels, dks, dvs = refs[3:8]
        combine(*refs[0:3], levels)
        dqt[...] = jnp.zeros_like(dqt)
    else:
        before, levels, dkv, dq, dqt, dks, dvs, dqs = refs
        dqt[...] = before[...]
    dks[...] = jnp.zeros_like(dks)
    dvs[...] = jnp.zeros_like(dvs)
    for n in range(QROWS // QCHUNK):
        rows = slice(n * QCHUNK, (n + 1) * QCHUNK)

        def step(keys, _):
            group = kgrp[keys, :]
            ok = jnp.concatenate([group] * (QCHUNK // HD), axis=1) <= qgrp[0:1, rows]
            for h in range(HEADS):
                cols = slice(h * HD, (h + 1) * HD)
                key = kbuf[0, keys, cols]
                query = qbuf[0, rows, cols]
                grad = qbuf[1, rows, cols]
                scores = dot(key, query, NT)
                dprobs = dot(kbuf[1, keys, cols], grad, NT)
                scores = jnp.where(ok, scores * (SCALE * LOG2E), NEG)
                probs = jnp.exp2(scores - levels[h : h + 1, rows])
                dscores = (probs * (dprobs - levels[3 + h : 4 + h, rows])).astype(jnp.bfloat16)
                dvs[keys, cols] += dot(probs.astype(jnp.bfloat16), grad, NN)
                dks[keys, cols] += dot(dscores, query, NN)
                dqt[h, :, rows] += dot(key, dscores, TN)
            return 0

        visit(blocks[n], step, 0)
    row = lax.broadcasted_iota(jnp.int32, (PART, COLS), 0)
    for j in range(4):
        for s in range(4):
            rows = aligned(k_first[j][s])
            live = row < k_live[j][s]
            dkv[s, j, 0] = jnp.where(live, dks[rows, :] * SCALE, 0.0).astype(jnp.bfloat16)
            dkv[s, j, 1] = jnp.where(live, dvs[rows, :], 0.0).astype(jnp.bfloat16)
    if o == 0:
        for h in range(HEADS):
            dqs[:, h * HD : (h + 1) * HD] = (dqt[h] * SCALE).T
        for s in range(4):
            for j in range(4):
                n = s * 4 + j
                rows = aligned(q_first[n])
                dq[s, j] = jnp.where(row < q_live[n], dqs[rows, :], 0.0).astype(jnp.bfloat16)


SMEM = pl.BlockSpec(memory_space=pltpu.SMEM)
VMEM = pl.BlockSpec(memory_space=pltpu.VMEM)
PARAMS = pltpu.CompilerParams(vmem_limit_bytes=48 * 1024 * 1024)


def run(kernel, name, out_shape, tables, arrays, scratch=()):
    return pl.pallas_call(
        kernel,
        out_shape=out_shape,
        in_specs=[SMEM] * len(tables) + [VMEM] * len(arrays),
        out_specs=(VMEM,) * len(out_shape),
        scratch_shapes=list(scratch),
        compiler_params=PARAMS,
        cost_estimate=pl.CostEstimate(flops=3 * 10**9, bytes_accessed=6 * 10**6, transcendentals=2 * 10**6),
        name=name,
    )(*tables, *arrays)


def local(query, keys, values, dout, slot_group, valid):
    c = lax.axis_index("head") % NC
    bf16, f32 = jnp.bfloat16, jnp.float32

    keep, give = pl.pallas_call(
        pack_kernel,
        out_shape=(jax.ShapeDtypeStruct((4, 4, SUB, COLS), bf16),) * 2,
        in_specs=[VMEM] * 4,
        out_specs=(VMEM,) * 2,
        name="pack",
    )(query, dout, keys, values)
    take = swap_core(give)
    both = jnp.where(c == 0, jnp.concatenate([keep, take], axis=2), jnp.concatenate([take, keep], axis=2))
    got = {j: send(both[j], lambda y, z, x, c: (y, z + c + 2 * j, x, c)) for j in (2, 1, 3, 0)}
    own_qd = jnp.stack([got[j][0:2] for j in range(4)])
    own_kv = jnp.stack([got[j][2:4] for j in range(4)])

    kv_first, qd_first = lax.optimization_barrier((first_x(own_kv), first_y(own_qd)))
    kv_rest = second_x(jnp.stack([own_kv, kv_first]))
    qd_rest = second_y(jnp.stack([own_qd, qd_first]))

    i32 = jnp.int32
    tables = (slot_group, valid)
    kbuf_type = jax.ShapeDtypeStruct((2, KROWS, COLS), bf16)
    kgrp_type = jax.ShapeDtypeStruct((KROWS, HD), i32)
    stats_type = jax.ShapeDtypeStruct((16, QROWS), f32)
    qbuf, qgrp, kbuf, kgrp, part = run(
        functools.partial(stats_kernel, 0),
        "stats_own",
        (jax.ShapeDtypeStruct((2, QROWS, COLS), bf16), jax.ShapeDtypeStruct((8, QROWS), i32))
        + (kbuf_type, kgrp_type, stats_type),
        tables,
        (own_qd, qd_first, qd_rest, own_kv, kv_first, kv_rest),
    )
    kbuf_other, kgrp_other, stats = run(
        functools.partial(stats_kernel, 1),
        "stats_other",
        (kbuf_type, kgrp_type, stats_type),
        tables,
        (qbuf, qgrp, part, swap_core(own_kv), swap_core(kv_first), swap_core(kv_rest)),
    )

    stats_first = first_y(stats)
    stats_rest = second_y(jnp.stack([stats, stats_first]))

    dkv_type = jax.ShapeDtypeStruct((4, 4, 2, PART, COLS), bf16)
    scratch = [
        pltpu.VMEM((HEADS, HD, QROWS), f32),
        pltpu.VMEM((KROWS, COLS), f32),
        pltpu.VMEM((KROWS, COLS), f32),
    ]
    dkv_other, dqt, levels = run(
        functools.partial(grad_kernel, 1),
        "grads_other",
        (
            dkv_type,
            jax.ShapeDtypeStruct((HEADS, HD, QROWS), f32),
            jax.ShapeDtypeStruct((8, QROWS), f32),
        ),
        tables,
        (qbuf, qgrp, kbuf_other, kgrp_other, stats, stats_first, stats_rest),
        scratch[1:],
    )
    swapped = swap_core(dkv_other)
    dkv_own, dq = run(
        functools.partial(grad_kernel, 0),
        "grads_own",
        (dkv_type, jax.ShapeDtypeStruct((4, 4, PART, COLS), bf16)),
        tables,
        (qbuf, qgrp, kbuf, kgrp, dqt, levels),
        scratch + [pltpu.VMEM((QROWS, COLS), f32)],
    )

    dkv_sum = dkv_own.astype(f32) + swapped.astype(f32)
    dkv_half, dq_half = lax.optimization_barrier((second_x(dkv_sum[2:4].astype(bf16)), second_y(dq[2:4])))
    dkv_sum = dkv_sum[0:2] + dkv_half.astype(f32)
    dq_sum = dq[0:2].astype(f32) + dq_half.astype(f32)
    dkv_last, dq_last = lax.optimization_barrier(
        (first_x(dkv_sum[1].astype(bf16)), first_y(dq_sum[1].astype(bf16)))
    )
    dkv_sum = (dkv_sum[0] + dkv_last.astype(f32)).astype(bf16)
    dq_sum = (dq_sum[0] + dq_last.astype(f32)).astype(bf16)

    back = {}
    for j in (2, 1, 3, 0):
        block = jnp.concatenate([dq_sum[j][None], dkv_sum[j]], axis=0)
        back[j] = send(block, lambda y, z, x, c: (y, z - c - 2 * j, x, c))
    back = [back[j] for j in range(4)]
    first = jnp.stack([b[:, :SUB] for b in back])
    second = jnp.stack([b[:, SUB:] for b in back])
    theirs = swap_core(jnp.where(c == 0, second, first))
    return pl.pallas_call(
        unpack_kernel,
        out_shape=(jax.ShapeDtypeStruct((SUB, NZ * COLS), bf16),) * 3,
        in_specs=[VMEM] * 2,
        out_specs=(VMEM,) * 3,
        name="unpack",
    )(jnp.where(c == 0, first, second), theirs)


def solution(mesh):
    spec = P(("tm", "head"), None)
    return jax.shard_map(
        local,
        mesh=mesh,
        in_specs=(spec, spec, spec, spec, P(), P()),
        out_specs=(spec, spec, spec),
        check_vma=False,
    )
```

```python
import functools
import math

import jax
import jax.numpy as jnp
from jax import lax
from jax.experimental import pallas as pl
from jax.experimental.pallas import tpu as pltpu
from jax.sharding import PartitionSpec as P

HD = 128
HEADS = 3
COLS = HEADS * HD
NY, NZ, NX, NC = 4, 8, 4, 2
PART = 48
SUB = 24
QROWS = 768
NEG = -1e30
LOW = -1e29
FAR = 1000
SCALE = 1.0 / math.sqrt(HD)
LOG2E = 1.4426950408889634
QCHUNK = 256
KROWS = 768
KCHUNK = 512

NT = (((1,), (1,)), ((), ()))
NN = (((1,), (0,)), ((), ()))
TN = (((0,), (0,)), ((), ()))


def pairs(move):
    out = []
    for y in range(NY):
        for z in range(NZ):
            for x in range(NX):
                for c in range(NC):
                    ty, tz, tx, tc = move(y, z, x, c)
                    ty, tz, tx = ty % NY, tz % NZ, tx % NX
                    out.append((((y * NZ + z) * NX + x) * NC + c, ((ty * NZ + tz) * NX + tx) * NC + tc))
    return out


def send(array, move):
    return lax.ppermute(array, ("tm", "head"), pairs(move))


def swap_core(array):
    return send(array, lambda y, z, x, c: (y, z, x, 1 - c))


def dot(a, b, dims):
    return lax.dot_general(a, b, dims, preferred_element_type=jnp.float32)


def position():
    tm = lax.axis_index("tm")
    head = lax.axis_index("head")
    return tm // NZ, tm % NZ, head // NC, head % NC


def pack_kernel(query, grad, keys, values, keep, give):
    _, z, _, c = position()
    for j in range(4):
        mine = pl.ds(pl.multiple_of(((z + c + 2 * j) & 7) * COLS, HD), COLS)
        theirs = pl.ds(pl.multiple_of(((z + 1 - c + 2 * j) & 7) * COLS, HD), COLS)
        for n, array in enumerate((query, grad, keys, values)):
            keep[j, n] = array[:, mine]
            give[j, n] = array[:, theirs]


def unpack_kernel(mine, theirs, *outs):
    _, z, _, c = position()
    for j in range(4):
        own = pl.ds(pl.multiple_of(((z + c + 2 * j) & 7) * COLS, HD), COLS)
        other = pl.ds(pl.multiple_of(((z + 1 - c + 2 * j) & 7) * COLS, HD), COLS)
        for n in range(3):
            outs[n][:, own] = mine[j, n]
            outs[n][:, other] = theirs[j, n]


def flip(s, core):
    return (0, 1 + 2 * core, 3 - 2 * core, 2)[s]


def query_slot(at, s, j):
    return (at[0] ^ flip(s, at[3])) * NZ + ((at[1] - at[3] - 2 * j) & 7)


def key_slot(at, o, j):
    core = 1 - at[3] if o else at[3]
    return at[0] * NZ + ((at[1] - core - 2 * j) & 7)


def key_part(at, o, s):
    return at[2] ^ flip(s, 1 - at[3] if o else at[3])


def first_y(array):
    return send(array, lambda y, z, x, c: (y ^ (1 + 2 * c), z, x, c))


def second_y(array):
    return send(array, lambda y, z, x, c: (y ^ (3 - 2 * c), z, x, c))


def first_x(array):
    return send(array, lambda y, z, x, c: (y, z, x ^ (1 + 2 * c), c))


def second_x(array):
    return send(array, lambda y, z, x, c: (y, z, x ^ (3 - 2 * c), c))


def pieces(own, first, rest):
    return (own, first, rest.at[0], rest.at[1])


def clip_rows(count):
    return jnp.minimum(jnp.maximum(count, 0), PART)


def round_rows(count):
    return ((count + 15) // 16) * 16


def place_queries(at, groups, valid):
    group = [groups[query_slot(at, s, j)] for s in range(4) for j in range(4)]
    live = [clip_rows(valid[g] - PART * at[2]) for g in group]
    padded = [round_rows(n) for n in live]
    first = [sum(jnp.where(other < mine, n, 0) for other, n in zip(group, padded)) for mine in group]
    tops = []
    for n in range(QROWS // QCHUNK):
        inside = [
            jnp.where((f < QCHUNK * (n + 1)) & (count > 0), g, -1) for g, f, count in zip(group, first, live)
        ]
        tops.append(jnp.where(sum(padded) > QCHUNK * n, functools.reduce(jnp.maximum, inside), -1))
    return group, live, first, tops


def place_keys(at, groups, valid, o, tops):
    group = [groups[key_slot(at, o, j)] for j in range(4)]
    rows = [round_rows(valid[g]) for g in group]
    first, live = [], []
    for mine in group:
        here = sum(jnp.where(other < mine, n, 0) for other, n in zip(group, rows))
        firsts, lives = [], []
        for s in range(4):
            count = clip_rows(valid[mine] - PART * key_part(at, o, s))
            firsts.append(here)
            lives.append(count)
            here = here + round_rows(count)
        first.append(firsts)
        live.append(lives)
    half = KCHUNK // 2
    blocks = []
    for top in tops:
        seen = sum(jnp.where(g <= top, n, 0) for g, n in zip(group, rows))
        blocks.append((seen + half - 1) // half)
    return group, live, first, blocks


def pick(values, n):
    out = values[-1]
    for i in range(len(values) - 1):
        out = jnp.where(n == i, values[i], out)
    return out


def visit(blocks, step, state):
    half = KCHUNK // 2
    whole = blocks // 2
    state = lax.fori_loop(0, whole, lambda i, v: step(pl.ds(pl.multiple_of(i * KCHUNK, KCHUNK), KCHUNK), v), state)
    return lax.fori_loop(
        0, blocks - 2 * whole, lambda i, v: step(pl.ds(pl.multiple_of(whole * KCHUNK, KCHUNK), half), v), state
    )


def aligned(first):
    return pl.ds(pl.multiple_of(first, 16), PART)


def load_queries(qd, qbuf, qgrp, q_group, q_live, q_first):
    qbuf[...] = jnp.zeros_like(qbuf)
    row = lax.broadcasted_iota(jnp.int32, (PART, COLS), 0)
    lane = lax.broadcasted_iota(jnp.int32, (8, QROWS), 1)
    lane_group = jnp.full((8, QROWS), -1, jnp.int32)
    for s in range(4):
        for j in range(4):
            n = s * 4 + j
            rows = aligned(q_first[n])
            live = row < q_live[n]
            for a in range(2):
                qbuf[a, rows, :] = jnp.where(live, qd[s][j, a], qbuf[a, rows, :])
            here = (lane >= q_first[n]) & (lane < q_first[n] + q_live[n])
            lane_group = jnp.where(here, q_group[n], lane_group)
    qgrp[...] = lane_group


def load_keys(kv, kbuf, kgrp, k_group, k_live, k_first):
    kbuf[...] = jnp.zeros_like(kbuf)
    kgrp[...] = jnp.full_like(kgrp, FAR)
    row = lax.broadcasted_iota(jnp.int32, (PART, COLS), 0)
    row_lanes = lax.broadcasted_iota(jnp.int32, (PART, HD), 0)
    for j in range(4):
        for s in range(4):
            rows = aligned(k_first[j][s])
            live = row < k_live[j][s]
            for a in range(2):
                kbuf[a, rows, :] = jnp.where(live, kv[s][j, a], kbuf[a, rows, :])
            kgrp[rows, :] = jnp.where(row_lanes < k_live[j][s], k_group[j], kgrp[rows, :])


def stats_kernel(o, groups, valid, *refs):
    at = position()
    q_group, q_live, q_first, tops = place_queries(at, groups, valid)
    k_group, k_live, k_first, blocks = place_keys(at, groups, valid, o, tops)
    if o == 0:
        qbuf, qgrp, kbuf, kgrp, stats = refs[6:11]
        load_queries(pieces(*refs[0:3]), qbuf, qgrp, q_group, q_live, q_first)
    else:
        qbuf, qgrp, before = refs[0:3]
        kbuf, kgrp, stats = refs[6:9]
    load_keys(pieces(*refs[3:6]), kbuf, kgrp, k_group, k_live, k_first)
    stats[...] = jnp.zeros_like(stats)
    def chunk(n, _):
        rows = pl.ds(pl.multiple_of(n * QCHUNK, QCHUNK), QCHUNK)

        def step(keys, carry):
            group = kgrp[keys, :]
            ok = jnp.concatenate([group] * (QCHUNK // HD), axis=1) <= qgrp[0:1, rows]
            out = []
            for h in range(HEADS):
                cols = slice(h * HD, (h + 1) * HD)
                top, total, weighted = carry[h]
                scores = dot(kbuf[0, keys, cols], qbuf[0, rows, cols], NT)
                dprobs = dot(kbuf[1, keys, cols], qbuf[1, rows, cols], NT)
                scores = jnp.where(ok, scores * (SCALE * LOG2E), NEG)
                new_top = jnp.maximum(top, jnp.max(scores, axis=0, keepdims=True))
                weights = jnp.exp2(scores - new_top)
                factor = jnp.exp2(top - new_top)
                total = total * factor + jnp.sum(weights, axis=0, keepdims=True)
                weighted = weighted * factor + jnp.sum(weights * dprobs, axis=0, keepdims=True)
                out.append((new_top, total, weighted))
            return tuple(out)

        if o == 0:
            start = (
                jnp.full((1, QCHUNK), LOW, jnp.float32),
                jnp.zeros((1, QCHUNK), jnp.float32),
                jnp.zeros((1, QCHUNK), jnp.float32),
            )
            start = (start,) * HEADS
        else:
            start = tuple(
                tuple(before[3 * k + h : 3 * k + h + 1, rows] for k in range(3)) for h in range(HEADS)
            )
        final = visit(pick(blocks, n), step, start)
        for h in range(HEADS):
            for k in range(3):
                stats[3 * k + h : 3 * k + h + 1, rows] = final[h][k]
        return 0

    lax.fori_loop(0, QROWS // QCHUNK, chunk, 0)


def combine(st0, st1, st23, levels):
    sts = [st0[...], st1[...], st23[0], st23[1]]
    top = functools.reduce(jnp.maximum, [st[0:3, :] for st in sts])
    factors = [jnp.exp2(st[0:3, :] - top) for st in sts]
    total = sum(f * st[3:6, :] for f, st in zip(factors, sts))
    weighted = sum(f * st[6:9, :] for f, st in zip(factors, sts))
    some = total > 0.0
    safe = jnp.where(some, total, 1.0)
    levels[0:3, :] = jnp.where(some, top + jnp.log2(safe), 0.0)
    levels[3:6, :] = weighted / safe
    levels[6:8, :] = jnp.zeros_like(levels[6:8, :])


def grad_kernel(o, groups, valid, qbuf, qgrp, kbuf, kgrp, *refs):
    at = position()
    q_group, q_live, q_first, tops = place_queries(at, groups, valid)
    k_group, k_live, k_first, blocks = place_keys(at, groups, valid, o, tops)
    if o == 1:
        dkv, dqt, levels, dks, dvs = refs[3:8]
        combine(*refs[0:3], levels)
        dqt[...] = jnp.zeros_like(dqt)
    else:
        before, levels, dkv, dq, dqt, dks, dvs, dqs = refs
        dqt[...] = before[...]
    dks[...] = jnp.zeros_like(dks)
    dvs[...] = jnp.zeros_like(dvs)

    def chunk(n, _):
        rows = pl.ds(pl.multiple_of(n * QCHUNK, QCHUNK), QCHUNK)

        def step(keys, _):
            group = kgrp[keys, :]
            ok = jnp.concatenate([group] * (QCHUNK // HD), axis=1) <= qgrp[0:1, rows]
            for h in range(HEADS):
                cols = slice(h * HD, (h + 1) * HD)
                key = kbuf[0, keys, cols]
                query = qbuf[0, rows, cols]
                grad = qbuf[1, rows, cols]
                scores = dot(key, query, NT)
                dprobs = dot(kbuf[1, keys, cols], grad, NT)
                scores = jnp.where(ok, scores * (SCALE * LOG2E), NEG)
                probs = jnp.exp2(scores - levels[h : h + 1, rows])
                dscores = (probs * (dprobs - levels[3 + h : 4 + h, rows])).astype(jnp.bfloat16)
                dvs[keys, cols] += dot(probs.astype(jnp.bfloat16), grad, NN)
                dks[keys, cols] += dot(dscores, query, NN)
                dqt[h, :, rows] += dot(key, dscores, TN)
            return 0

        visit(pick(blocks, n), step, 0)
        return 0

    lax.fori_loop(0, QROWS // QCHUNK, chunk, 0)
    row = lax.broadcasted_iota(jnp.int32, (PART, COLS), 0)
    for j in range(4):
        for s in range(4):
            rows = aligned(k_first[j][s])
            live = row < k_live[j][s]
            dkv[s, j, 0] = jnp.where(live, dks[rows, :] * SCALE, 0.0).astype(jnp.bfloat16)
            dkv[s, j, 1] = jnp.where(live, dvs[rows, :], 0.0).astype(jnp.bfloat16)
    if o == 0:
        for h in range(HEADS):
            dqs[:, h * HD : (h + 1) * HD] = (dqt[h] * SCALE).T
        for s in range(4):
            for j in range(4):
                n = s * 4 + j
                rows = aligned(q_first[n])
                dq[s, j] = jnp.where(row < q_live[n], dqs[rows, :], 0.0).astype(jnp.bfloat16)


SMEM = pl.BlockSpec(memory_space=pltpu.SMEM)
VMEM = pl.BlockSpec(memory_space=pltpu.VMEM)
PARAMS = pltpu.CompilerParams(vmem_limit_bytes=48 * 1024 * 1024)


def run(kernel, name, out_shape, tables, arrays, scratch=()):
    return pl.pallas_call(
        kernel,
        out_shape=out_shape,
        in_specs=[SMEM] * len(tables) + [VMEM] * len(arrays),
        out_specs=(VMEM,) * len(out_shape),
        scratch_shapes=list(scratch),
        compiler_params=PARAMS,
        cost_estimate=pl.CostEstimate(flops=3 * 10**9, bytes_accessed=6 * 10**6, transcendentals=2 * 10**6),
        name=name,
    )(*tables, *arrays)


def local(query, keys, values, dout, slot_group, valid):
    c = lax.axis_index("head") % NC
    bf16, f32 = jnp.bfloat16, jnp.float32

    keep, give = pl.pallas_call(
        pack_kernel,
        out_shape=(jax.ShapeDtypeStruct((4, 4, SUB, COLS), bf16),) * 2,
        in_specs=[VMEM] * 4,
        out_specs=(VMEM,) * 2,
        name="pack",
    )(query, dout, keys, values)
    take = swap_core(give)
    both = jnp.where(c == 0, jnp.concatenate([keep, take], axis=2), jnp.concatenate([take, keep], axis=2))
    got = {j: send(both[j], lambda y, z, x, c: (y, z + c + 2 * j, x, c)) for j in (2, 1, 3, 0)}
    own_qd = jnp.stack([got[j][0:2] for j in range(4)])
    own_kv = jnp.stack([got[j][2:4] for j in range(4)])

    kv_first, qd_first = lax.optimization_barrier((first_x(own_kv), first_y(own_qd)))
    kv_rest = second_x(jnp.stack([own_kv, kv_first]))
    qd_rest = second_y(jnp.stack([own_qd, qd_first]))

    i32 = jnp.int32
    tables = (slot_group, valid)
    kbuf_type = jax.ShapeDtypeStruct((2, KROWS, COLS), bf16)
    kgrp_type = jax.ShapeDtypeStruct((KROWS, HD), i32)
    stats_type = jax.ShapeDtypeStruct((16, QROWS), f32)
    qbuf, qgrp, kbuf, kgrp, part = run(
        functools.partial(stats_kernel, 0),
        "stats_own",
        (jax.ShapeDtypeStruct((2, QROWS, COLS), bf16), jax.ShapeDtypeStruct((8, QROWS), i32))
        + (kbuf_type, kgrp_type, stats_type),
        tables,
        (own_qd, qd_first, qd_rest, own_kv, kv_first, kv_rest),
    )
    kbuf_other, kgrp_other, stats = run(
        functools.partial(stats_kernel, 1),
        "stats_other",
        (kbuf_type, kgrp_type, stats_type),
        tables,
        (qbuf, qgrp, part, swap_core(own_kv), swap_core(kv_first), swap_core(kv_rest)),
    )

    stats_first = first_y(stats)
    stats_rest = second_y(jnp.stack([stats, stats_first]))

    dkv_type = jax.ShapeDtypeStruct((4, 4, 2, PART, COLS), bf16)
    scratch = [
        pltpu.VMEM((HEADS, HD, QROWS), f32),
        pltpu.VMEM((KROWS, COLS), f32),
        pltpu.VMEM((KROWS, COLS), f32),
    ]
    dkv_other, dqt, levels = run(
        functools.partial(grad_kernel, 1),
        "grads_other",
        (
            dkv_type,
            jax.ShapeDtypeStruct((HEADS, HD, QROWS), f32),
            jax.ShapeDtypeStruct((8, QROWS), f32),
        ),
        tables,
        (qbuf, qgrp, kbuf_other, kgrp_other, stats, stats_first, stats_rest),
        scratch[1:],
    )
    swapped = swap_core(dkv_other)
    dkv_own, dq = run(
        functools.partial(grad_kernel, 0),
        "grads_own",
        (dkv_type, jax.ShapeDtypeStruct((4, 4, PART, COLS), bf16)),
        tables,
        (qbuf, qgrp, kbuf, kgrp, dqt, levels),
        scratch + [pltpu.VMEM((QROWS, COLS), f32)],
    )

    dkv_sum = dkv_own.astype(f32) + swapped.astype(f32)
    dkv_half, dq_half = lax.optimization_barrier((second_x(dkv_sum[2:4].astype(bf16)), second_y(dq[2:4])))
    dkv_sum = dkv_sum[0:2] + dkv_half.astype(f32)
    dq_sum = dq[0:2].astype(f32) + dq_half.astype(f32)
    dkv_last, dq_last = lax.optimization_barrier(
        (first_x(dkv_sum[1].astype(bf16)), first_y(dq_sum[1].astype(bf16)))
    )
    dkv_sum = (dkv_sum[0] + dkv_last.astype(f32)).astype(bf16)
    dq_sum = (dq_sum[0] + dq_last.astype(f32)).astype(bf16)

    back = {}
    for j in (2, 1, 3, 0):
        block = jnp.concatenate([dq_sum[j][None], dkv_sum[j]], axis=0)
        back[j] = send(block, lambda y, z, x, c: (y, z - c - 2 * j, x, c))
    back = [back[j] for j in range(4)]
    first = jnp.stack([b[:, :SUB] for b in back])
    second = jnp.stack([b[:, SUB:] for b in back])
    theirs = swap_core(jnp.where(c == 0, second, first))
    return pl.pallas_call(
        unpack_kernel,
        out_shape=(jax.ShapeDtypeStruct((SUB, NZ * COLS), bf16),) * 3,
        in_specs=[VMEM] * 2,
        out_specs=(VMEM,) * 3,
        name="unpack",
    )(jnp.where(c == 0, first, second), theirs)


def solution(mesh):
    spec = P(("tm", "head"), None)
    return jax.shard_map(
        local,
        mesh=mesh,
        in_specs=(spec, spec, spec, spec, P(), P()),
        out_specs=(spec, spec, spec),
        check_vma=False,
    )
```

```python
import functools
import math

import jax
import jax.numpy as jnp
from jax import lax
from jax.experimental import pallas as pl
from jax.experimental.pallas import tpu as pltpu
from jax.sharding import PartitionSpec as P

HD = 128
HEADS = 3
COLS = HEADS * HD
NY, NZ, NX, NC = 4, 8, 4, 2
PART = 48
SUB = 24
QROWS = 768
NEG = -1e30
LOW = -1e29
FAR = 1000
SCALE = 1.0 / math.sqrt(HD)
LOG2E = 1.4426950408889634
QCHUNK = 256
KROWS = 768
KCHUNK = 512

NT = (((1,), (1,)), ((), ()))
NN = (((1,), (0,)), ((), ()))
TN = (((0,), (0,)), ((), ()))


def pairs(move):
    out = []
    for y in range(NY):
        for z in range(NZ):
            for x in range(NX):
                for c in range(NC):
                    ty, tz, tx, tc = move(y, z, x, c)
                    ty, tz, tx = ty % NY, tz % NZ, tx % NX
                    out.append((((y * NZ + z) * NX + x) * NC + c, ((ty * NZ + tz) * NX + tx) * NC + tc))
    return out


def send(array, move):
    return lax.ppermute(array, ("tm", "head"), pairs(move))


def swap_core(array):
    return send(array, lambda y, z, x, c: (y, z, x, 1 - c))


def dot(a, b, dims):
    return lax.dot_general(a, b, dims, preferred_element_type=jnp.float32)


def position():
    tm = lax.axis_index("tm")
    head = lax.axis_index("head")
    return tm // NZ, tm % NZ, head // NC, head % NC


def pack_kernel(query, grad, keys, values, keep, give, rows, sems):
    _, z, _, c = position()
    copies = [
        pltpu.make_async_copy(array, rows.at[n], sems.at[n])
        for n, array in enumerate((query, grad, keys, values))
    ]
    for copy in copies:
        copy.start()
    for copy in copies:
        copy.wait()
    for j in range(4):
        mine = pl.ds(pl.multiple_of(((z + c + 2 * j) & 7) * COLS, HD), COLS)
        theirs = pl.ds(pl.multiple_of(((z + 1 - c + 2 * j) & 7) * COLS, HD), COLS)
        for n in range(4):
            keep[j, n] = rows[n, :, mine]
            give[j, n] = rows[n, :, theirs]


def unpack_kernel(mine, theirs, *outs):
    _, z, _, c = position()
    for j in range(4):
        own = pl.ds(pl.multiple_of(((z + c + 2 * j) & 7) * COLS, HD), COLS)
        other = pl.ds(pl.multiple_of(((z + 1 - c + 2 * j) & 7) * COLS, HD), COLS)
        for n in range(3):
            outs[n][:, own] = mine[j, n]
            outs[n][:, other] = theirs[j, n]


def flip(s, core):
    return (0, 1 + 2 * core, 3 - 2 * core, 2)[s]


def query_slot(at, s, j):
    return (at[0] ^ flip(s, at[3])) * NZ + ((at[1] - at[3] - 2 * j) & 7)


def key_slot(at, o, j):
    core = 1 - at[3] if o else at[3]
    return at[0] * NZ + ((at[1] - core - 2 * j) & 7)


def key_part(at, o, s):
    return at[2] ^ flip(s, 1 - at[3] if o else at[3])


def first_y(array):
    return send(array, lambda y, z, x, c: (y ^ (1 + 2 * c), z, x, c))


def second_y(array):
    return send(array, lambda y, z, x, c: (y ^ (3 - 2 * c), z, x, c))


def first_x(array):
    return send(array, lambda y, z, x, c: (y, z, x ^ (1 + 2 * c), c))


def second_x(array):
    return send(array, lambda y, z, x, c: (y, z, x ^ (3 - 2 * c), c))


def pieces(own, first, rest):
    return (own, first, rest.at[0], rest.at[1])


def clip_rows(count):
    return jnp.minimum(jnp.maximum(count, 0), PART)


def round_rows(count):
    return ((count + 15) // 16) * 16


def place_queries(at, groups, valid):
    group = [groups[query_slot(at, s, j)] for s in range(4) for j in range(4)]
    live = [clip_rows(valid[g] - PART * at[2]) for g in group]
    padded = [round_rows(n) for n in live]
    first = [sum(jnp.where(other < mine, n, 0) for other, n in zip(group, padded)) for mine in group]
    tops = []
    for n in range(QROWS // QCHUNK):
        inside = [
            jnp.where((f < QCHUNK * (n + 1)) & (count > 0), g, -1) for g, f, count in zip(group, first, live)
        ]
        tops.append(jnp.where(sum(padded) > QCHUNK * n, functools.reduce(jnp.maximum, inside), -1))
    return group, live, first, tops


def place_keys(at, groups, valid, o, tops):
    group = [groups[key_slot(at, o, j)] for j in range(4)]
    rows = [round_rows(valid[g]) for g in group]
    first, live = [], []
    for mine in group:
        here = sum(jnp.where(other < mine, n, 0) for other, n in zip(group, rows))
        firsts, lives = [], []
        for s in range(4):
            count = clip_rows(valid[mine] - PART * key_part(at, o, s))
            firsts.append(here)
            lives.append(count)
            here = here + round_rows(count)
        first.append(firsts)
        live.append(lives)
    half = KCHUNK // 2
    blocks = []
    for top in tops:
        seen = sum(jnp.where(g <= top, n, 0) for g, n in zip(group, rows))
        blocks.append((seen + half - 1) // half)
    return group, live, first, blocks


def pick(values, n):
    out = values[-1]
    for i in range(len(values) - 1):
        out = jnp.where(n == i, values[i], out)
    return out


def visit(blocks, step, state):
    half = KCHUNK // 2
    whole = blocks // 2
    state = lax.fori_loop(0, whole, lambda i, v: step(pl.ds(pl.multiple_of(i * KCHUNK, KCHUNK), KCHUNK), v), state)
    return lax.fori_loop(
        0, blocks - 2 * whole, lambda i, v: step(pl.ds(pl.multiple_of(whole * KCHUNK, KCHUNK), half), v), state
    )


def aligned(first):
    return pl.ds(pl.multiple_of(first, 16), PART)


def load_queries(qd, qbuf, qgrp, q_group, q_live, q_first):
    qbuf[...] = jnp.zeros_like(qbuf)
    row = lax.broadcasted_iota(jnp.int32, (PART, COLS), 0)
    lane = lax.broadcasted_iota(jnp.int32, (8, QROWS), 1)
    lane_group = jnp.full((8, QROWS), -1, jnp.int32)
    for s in range(4):
        for j in range(4):
            n = s * 4 + j
            rows = aligned(q_first[n])
            live = row < q_live[n]
            for a in range(2):
                qbuf[a, rows, :] = jnp.where(live, qd[s][j, a], qbuf[a, rows, :])
            here = (lane >= q_first[n]) & (lane < q_first[n] + q_live[n])
            lane_group = jnp.where(here, q_group[n], lane_group)
    qgrp[...] = lane_group


def load_keys(kv, kbuf, kgrp, k_group, k_live, k_first):
    kbuf[...] = jnp.zeros_like(kbuf)
    kgrp[...] = jnp.full_like(kgrp, FAR)
    row = lax.broadcasted_iota(jnp.int32, (PART, COLS), 0)
    row_lanes = lax.broadcasted_iota(jnp.int32, (PART, HD), 0)
    for j in range(4):
        for s in range(4):
            rows = aligned(k_first[j][s])
            live = row < k_live[j][s]
            for a in range(2):
                kbuf[a, rows, :] = jnp.where(live, kv[s][j, a], kbuf[a, rows, :])
            kgrp[rows, :] = jnp.where(row_lanes < k_live[j][s], k_group[j], kgrp[rows, :])


def stats_kernel(o, groups, valid, *refs):
    at = position()
    q_group, q_live, q_first, tops = place_queries(at, groups, valid)
    k_group, k_live, k_first, blocks = place_keys(at, groups, valid, o, tops)
    if o == 0:
        qbuf, qgrp, kbuf, kgrp, stats = refs[6:11]
        load_queries(pieces(*refs[0:3]), qbuf, qgrp, q_group, q_live, q_first)
    else:
        qbuf, qgrp, before = refs[0:3]
        kbuf, kgrp, stats = refs[6:9]
    load_keys(pieces(*refs[3:6]), kbuf, kgrp, k_group, k_live, k_first)
    stats[...] = jnp.zeros_like(stats)
    def chunk(n, _):
        rows = pl.ds(pl.multiple_of(n * QCHUNK, QCHUNK), QCHUNK)

        def step(keys, carry):
            group = kgrp[keys, :]
            ok = jnp.concatenate([group] * (QCHUNK // HD), axis=1) <= qgrp[0:1, rows]
            out = []
            for h in range(HEADS):
                cols = slice(h * HD, (h + 1) * HD)
                top, total, weighted = carry[h]
                scores = dot(kbuf[0, keys, cols], qbuf[0, rows, cols], NT)
                dprobs = dot(kbuf[1, keys, cols], qbuf[1, rows, cols], NT)
                scores = jnp.where(ok, scores * (SCALE * LOG2E), NEG)
                new_top = jnp.maximum(top, jnp.max(scores, axis=0, keepdims=True))
                weights = jnp.exp2(scores - new_top)
                factor = jnp.exp2(top - new_top)
                total = total * factor + jnp.sum(weights, axis=0, keepdims=True)
                weighted = weighted * factor + jnp.sum(weights * dprobs, axis=0, keepdims=True)
                out.append((new_top, total, weighted))
            return tuple(out)

        if o == 0:
            start = (
                jnp.full((1, QCHUNK), LOW, jnp.float32),
                jnp.zeros((1, QCHUNK), jnp.float32),
                jnp.zeros((1, QCHUNK), jnp.float32),
            )
            start = (start,) * HEADS
        else:
            start = tuple(
                tuple(before[3 * k + h : 3 * k + h + 1, rows] for k in range(3)) for h in range(HEADS)
            )
        final = visit(pick(blocks, n), step, start)
        for h in range(HEADS):
            for k in range(3):
                stats[3 * k + h : 3 * k + h + 1, rows] = final[h][k]
        return 0

    lax.fori_loop(0, QROWS // QCHUNK, chunk, 0)


def combine(parts, levels):
    sts = [st[...] for st in parts]
    top = functools.reduce(jnp.maximum, [st[0:3, :] for st in sts])
    factors = [jnp.exp2(st[0:3, :] - top) for st in sts]
    total = sum(f * st[3:6, :] for f, st in zip(factors, sts))
    weighted = sum(f * st[6:9, :] for f, st in zip(factors, sts))
    some = total > 0.0
    safe = jnp.where(some, total, 1.0)
    levels[0:3, :] = jnp.where(some, top + jnp.log2(safe), 0.0)
    levels[3:6, :] = weighted / safe
    levels[6:8, :] = jnp.zeros_like(levels[6:8, :])


def grad_kernel(o, groups, valid, qbuf, qgrp, kbuf, kgrp, *refs):
    at = position()
    q_group, q_live, q_first, tops = place_queries(at, groups, valid)
    k_group, k_live, k_first, blocks = place_keys(at, groups, valid, o, tops)
    if o == 1:
        dkv, dqt, levels, dks, dvs = refs[4:9]
        combine(refs[0:4], levels)
        dqt[...] = jnp.zeros_like(dqt)
    else:
        before, levels, dkv, dq, dqt, dks, dvs, dqs = refs
        dqt[...] = before[...]
    dks[...] = jnp.zeros_like(dks)
    dvs[...] = jnp.zeros_like(dvs)

    def chunk(n, _):
        rows = pl.ds(pl.multiple_of(n * QCHUNK, QCHUNK), QCHUNK)

        def step(keys, _):
            group = kgrp[keys, :]
            ok = jnp.concatenate([group] * (QCHUNK // HD), axis=1) <= qgrp[0:1, rows]
            products = []
            for h in range(HEADS):
                cols = slice(h * HD, (h + 1) * HD)
                scores = dot(kbuf[0, keys, cols], qbuf[0, rows, cols], NT)
                products.append((scores, dot(kbuf[1, keys, cols], qbuf[1, rows, cols], NT)))
            weights = []
            for h in range(HEADS):
                scores, dprobs = products[h]
                scores = jnp.where(ok, scores * (SCALE * LOG2E), NEG)
                probs = jnp.exp2(scores - levels[h : h + 1, rows])
                dscores = probs * (dprobs - levels[3 + h : 4 + h, rows])
                weights.append((probs.astype(jnp.bfloat16), dscores.astype(jnp.bfloat16)))
            for h in range(HEADS):
                cols = slice(h * HD, (h + 1) * HD)
                probs, dscores = weights[h]
                dvs[keys, cols] += dot(probs, qbuf[1, rows, cols], NN)
                dks[keys, cols] += dot(dscores, qbuf[0, rows, cols], NN)
                dqt[h, :, rows] += dot(kbuf[0, keys, cols], dscores, TN)
            return 0

        visit(pick(blocks, n), step, 0)
        return 0

    lax.fori_loop(0, QROWS // QCHUNK, chunk, 0)
    row = lax.broadcasted_iota(jnp.int32, (PART, COLS), 0)
    for j in range(4):
        for s in range(4):
            rows = aligned(k_first[j][s])
            live = row < k_live[j][s]
            dkv[s, j, 0] = jnp.where(live, dks[rows, :] * SCALE, 0.0).astype(jnp.bfloat16)
            dkv[s, j, 1] = jnp.where(live, dvs[rows, :], 0.0).astype(jnp.bfloat16)
    if o == 0:
        for h in range(HEADS):
            dqs[:, h * HD : (h + 1) * HD] = (dqt[h] * SCALE).T
        for s in range(4):
            for j in range(4):
                n = s * 4 + j
                rows = aligned(q_first[n])
                dq[s, j] = jnp.where(row < q_live[n], dqs[rows, :], 0.0).astype(jnp.bfloat16)


SMEM = pl.BlockSpec(memory_space=pltpu.SMEM)
VMEM = pl.BlockSpec(memory_space=pltpu.VMEM)
PARAMS = pltpu.CompilerParams(vmem_limit_bytes=24 * 1024 * 1024)
LARGE = pltpu.CompilerParams(vmem_limit_bytes=60 * 1024 * 1024)
SMALL = pltpu.CompilerParams(vmem_limit_bytes=6 * 1024 * 1024)


def run(kernel, name, out_shape, tables, arrays, scratch=()):
    return pl.pallas_call(
        kernel,
        out_shape=out_shape,
        in_specs=[SMEM] * len(tables) + [VMEM] * len(arrays),
        out_specs=(VMEM,) * len(out_shape),
        scratch_shapes=list(scratch),
        compiler_params=PARAMS,
        cost_estimate=pl.CostEstimate(flops=3 * 10**9, bytes_accessed=6 * 10**6, transcendentals=2 * 10**6),
        name=name,
    )(*tables, *arrays)


def local(query, keys, values, dout, slot_group, valid):
    c = lax.axis_index("head") % NC
    bf16, f32 = jnp.bfloat16, jnp.float32

    keep, give = pl.pallas_call(
        pack_kernel,
        out_shape=(jax.ShapeDtypeStruct((4, 4, SUB, COLS), bf16),) * 2,
        in_specs=[pl.BlockSpec(memory_space=pltpu.HBM)] * 4,
        out_specs=(VMEM,) * 2,
        scratch_shapes=[pltpu.VMEM((4, SUB, NZ * COLS), bf16), pltpu.SemaphoreType.DMA((4,))],
        compiler_params=LARGE,
        name="pack",
    )(query, dout, keys, values)
    take = swap_core(give)
    both = jnp.where(c == 0, jnp.concatenate([keep, take], axis=2), jnp.concatenate([take, keep], axis=2))
    got = {j: send(both[j], lambda y, z, x, c: (y, z + c + 2 * j, x, c)) for j in (2, 1, 3, 0)}
    own_qd = jnp.stack([got[j][0:2] for j in range(4)])
    own_kv = jnp.stack([got[j][2:4] for j in range(4)])

    kv_first, qd_first = lax.optimization_barrier((first_x(own_kv), first_y(own_qd)))
    kv_rest = second_x(jnp.stack([own_kv, kv_first]))
    qd_rest = second_y(jnp.stack([own_qd, qd_first]))

    i32 = jnp.int32
    tables = (slot_group, valid)
    kbuf_type = jax.ShapeDtypeStruct((2, KROWS, COLS), bf16)
    kgrp_type = jax.ShapeDtypeStruct((KROWS, HD), i32)
    stats_type = jax.ShapeDtypeStruct((16, QROWS), f32)
    qbuf, qgrp, kbuf, kgrp, part = run(
        functools.partial(stats_kernel, 0),
        "stats_own",
        (jax.ShapeDtypeStruct((2, QROWS, COLS), bf16), jax.ShapeDtypeStruct((8, QROWS), i32))
        + (kbuf_type, kgrp_type, stats_type),
        tables,
        (own_qd, qd_first, qd_rest, own_kv, kv_first, kv_rest),
    )
    kbuf_other, kgrp_other, stats = run(
        functools.partial(stats_kernel, 1),
        "stats_other",
        (kbuf_type, kgrp_type, stats_type),
        tables,
        (qbuf, qgrp, part, swap_core(own_kv), swap_core(kv_first), swap_core(kv_rest)),
    )

    all_stats = [stats] + [send(stats, lambda y, z, x, c: (y + n, z, x, c)) for n in (1, 2, 3)]

    dkv_type = jax.ShapeDtypeStruct((4, 4, 2, PART, COLS), bf16)
    scratch = [
        pltpu.VMEM((HEADS, HD, QROWS), f32),
        pltpu.VMEM((KROWS, COLS), f32),
        pltpu.VMEM((KROWS, COLS), f32),
    ]
    dkv_other, dqt, levels = run(
        functools.partial(grad_kernel, 1),
        "grads_other",
        (
            dkv_type,
            jax.ShapeDtypeStruct((HEADS, HD, QROWS), f32),
            jax.ShapeDtypeStruct((8, QROWS), f32),
        ),
        tables,
        (qbuf, qgrp, kbuf_other, kgrp_other, *all_stats),
        scratch[1:],
    )
    swapped = swap_core(dkv_other)
    dkv_own, dq = run(
        functools.partial(grad_kernel, 0),
        "grads_own",
        (dkv_type, jax.ShapeDtypeStruct((4, 4, PART, COLS), bf16)),
        tables,
        (qbuf, qgrp, kbuf, kgrp, dqt, levels),
        scratch + [pltpu.VMEM((QROWS, COLS), f32)],
    )

    dkv_sum = dkv_own.astype(f32) + swapped.astype(f32)
    dkv_half, dq_half = lax.optimization_barrier((second_x(dkv_sum[2:4].astype(bf16)), second_y(dq[2:4])))
    dkv_sum = dkv_sum[0:2] + dkv_half.astype(f32)
    dq_sum = dq[0:2].astype(f32) + dq_half.astype(f32)
    dkv_last, dq_last = lax.optimization_barrier(
        (first_x(dkv_sum[1].astype(bf16)), first_y(dq_sum[1].astype(bf16)))
    )
    dkv_sum = (dkv_sum[0] + dkv_last.astype(f32)).astype(bf16)
    dq_sum = (dq_sum[0] + dq_last.astype(f32)).astype(bf16)

    back = {}
    for j in (2, 1, 3, 0):
        block = jnp.concatenate([dq_sum[j][None], dkv_sum[j]], axis=0)
        back[j] = send(block, lambda y, z, x, c: (y, z - c - 2 * j, x, c))
    back = [back[j] for j in range(4)]
    first = jnp.stack([b[:, :SUB] for b in back])
    second = jnp.stack([b[:, SUB:] for b in back])
    theirs = swap_core(jnp.where(c == 0, second, first))
    return pl.pallas_call(
        unpack_kernel,
        out_shape=(jax.ShapeDtypeStruct((SUB, NZ * COLS), bf16),) * 3,
        in_specs=[VMEM] * 2,
        out_specs=(VMEM,) * 3,
        compiler_params=SMALL,
        name="unpack",
    )(jnp.where(c == 0, first, second), theirs)


def solution(mesh):
    spec = P(("tm", "head"), None)
    return jax.shard_map(
        local,
        mesh=mesh,
        in_specs=(spec, spec, spec, spec, P(), P()),
        out_specs=(spec, spec, spec),
        check_vma=False,
    )
```

```python
import functools
import math

import jax
import jax.numpy as jnp
from jax import lax
from jax.experimental import pallas as pl
from jax.experimental.pallas import tpu as pltpu
from jax.sharding import PartitionSpec as P

HD = 128
HEADS = 3
COLS = HEADS * HD
NY, NZ, NX, NC = 4, 8, 4, 2
PART = 48
SUB = 24
QROWS = 768
NEG = -1e30
LOW = -1e29
FAR = 1000
SCALE = 1.0 / math.sqrt(HD)
LOG2E = 1.4426950408889634
QCHUNK = 256
KROWS = 768
KCHUNK = 512

NT = (((1,), (1,)), ((), ()))
NN = (((1,), (0,)), ((), ()))
TN = (((0,), (0,)), ((), ()))


def pairs(move):
    out = []
    for y in range(NY):
        for z in range(NZ):
            for x in range(NX):
                for c in range(NC):
                    ty, tz, tx, tc = move(y, z, x, c)
                    ty, tz, tx = ty % NY, tz % NZ, tx % NX
                    out.append((((y * NZ + z) * NX + x) * NC + c, ((ty * NZ + tz) * NX + tx) * NC + tc))
    return out


def send(array, move):
    return lax.ppermute(array, ("tm", "head"), pairs(move))


def swap_core(array):
    return send(array, lambda y, z, x, c: (y, z, x, 1 - c))


def dot(a, b, dims):
    return lax.dot_general(a, b, dims, preferred_element_type=jnp.float32)


def position():
    tm = lax.axis_index("tm")
    head = lax.axis_index("head")
    return tm // NZ, tm % NZ, head // NC, head % NC


def pack_kernel(query, grad, keys, values, keep, give, rows, sems):
    _, z, _, c = position()
    copies = [
        pltpu.make_async_copy(array, rows.at[n], sems.at[n])
        for n, array in enumerate((query, grad, keys, values))
    ]
    for copy in copies:
        copy.start()
    for copy in copies:
        copy.wait()
    for j in range(4):
        mine = pl.ds(pl.multiple_of(((z + c + 2 * j) & 7) * COLS, HD), COLS)
        theirs = pl.ds(pl.multiple_of(((z + 1 - c + 2 * j) & 7) * COLS, HD), COLS)
        for n in range(4):
            keep[j, n] = rows[n, :, mine]
            give[j, n] = rows[n, :, theirs]


def unpack_kernel(mine, theirs, *outs):
    _, z, _, c = position()
    for j in range(4):
        own = pl.ds(pl.multiple_of(((z + c + 2 * j) & 7) * COLS, HD), COLS)
        other = pl.ds(pl.multiple_of(((z + 1 - c + 2 * j) & 7) * COLS, HD), COLS)
        for n in range(3):
            outs[n][:, own] = mine[j, n]
            outs[n][:, other] = theirs[j, n]


def flip(s, core):
    return (0, 1 + 2 * core, 3 - 2 * core, 2)[s]


def query_slot(at, s, j):
    return (at[0] ^ flip(s, at[3])) * NZ + ((at[1] - at[3] - 2 * j) & 7)


def key_slot(at, o, j):
    core = 1 - at[3] if o else at[3]
    return at[0] * NZ + ((at[1] - core - 2 * j) & 7)


def key_part(at, o, s):
    return at[2] ^ flip(s, 1 - at[3] if o else at[3])


def first_y(array):
    return send(array, lambda y, z, x, c: (y ^ (1 + 2 * c), z, x, c))


def second_y(array):
    return send(array, lambda y, z, x, c: (y ^ (3 - 2 * c), z, x, c))


def first_x(array):
    return send(array, lambda y, z, x, c: (y, z, x ^ (1 + 2 * c), c))


def second_x(array):
    return send(array, lambda y, z, x, c: (y, z, x ^ (3 - 2 * c), c))


def pieces(own, first, rest):
    return (own, first, rest.at[0], rest.at[1])


def clip_rows(count):
    return jnp.minimum(jnp.maximum(count, 0), PART)


def round_rows(count):
    return ((count + 15) // 16) * 16


def place_queries(at, groups, valid):
    group = [groups[query_slot(at, s, j)] for s in range(4) for j in range(4)]
    live = [clip_rows(valid[g] - PART * at[2]) for g in group]
    padded = [round_rows(n) for n in live]
    first = [sum(jnp.where(other < mine, n, 0) for other, n in zip(group, padded)) for mine in group]
    tops = []
    for n in range(QROWS // QCHUNK):
        inside = [
            jnp.where((f < QCHUNK * (n + 1)) & (count > 0), g, -1) for g, f, count in zip(group, first, live)
        ]
        tops.append(jnp.where(sum(padded) > QCHUNK * n, functools.reduce(jnp.maximum, inside), -1))
    return group, live, first, tops


def place_keys(at, groups, valid, o, tops):
    group = [groups[key_slot(at, o, j)] for j in range(4)]
    rows = [round_rows(valid[g]) for g in group]
    first, live = [], []
    for mine in group:
        here = sum(jnp.where(other < mine, n, 0) for other, n in zip(group, rows))
        firsts, lives = [], []
        for s in range(4):
            count = clip_rows(valid[mine] - PART * key_part(at, o, s))
            firsts.append(here)
            lives.append(count)
            here = here + round_rows(count)
        first.append(firsts)
        live.append(lives)
    half = KCHUNK // 2
    blocks = []
    for top in tops:
        seen = sum(jnp.where(g <= top, n, 0) for g, n in zip(group, rows))
        blocks.append((seen + half - 1) // half)
    return group, live, first, blocks


def table_kernel(groups, valid, table):
    at = position()
    q_group, q_live, q_first, tops = place_queries(at, groups, valid)
    for n in range(16):
        table[n] = q_group[n]
        table[16 + n] = q_live[n]
        table[32 + n] = q_first[n]
    for o in range(2):
        k_group, k_live, k_first, blocks = place_keys(at, groups, valid, o, tops)
        for j in range(4):
            table[48 + 4 * o + j] = k_group[j]
            for s in range(4):
                table[56 + 16 * o + 4 * j + s] = k_live[j][s]
                table[88 + 16 * o + 4 * j + s] = k_first[j][s]
        for n in range(QROWS // QCHUNK):
            table[120 + 3 * o + n] = blocks[n]
    table[126] = 0
    table[127] = 0


def read_queries(table):
    return tuple([table[first + n] for n in range(16)] for first in (0, 16, 32))


def read_keys(table, o):
    group = [table[48 + 4 * o + j] for j in range(4)]
    live = [[table[56 + 16 * o + 4 * j + s] for s in range(4)] for j in range(4)]
    first = [[table[88 + 16 * o + 4 * j + s] for s in range(4)] for j in range(4)]
    return group, live, first, [table[120 + 3 * o + n] for n in range(QROWS // QCHUNK)]


def pick(values, n):
    out = values[-1]
    for i in range(len(values) - 1):
        out = jnp.where(n == i, values[i], out)
    return out


def visit(blocks, step, state):
    half = KCHUNK // 2
    whole = blocks // 2
    state = lax.fori_loop(0, whole, lambda i, v: step(pl.ds(pl.multiple_of(i * KCHUNK, KCHUNK), KCHUNK), v), state)
    return lax.fori_loop(
        0, blocks - 2 * whole, lambda i, v: step(pl.ds(pl.multiple_of(whole * KCHUNK, KCHUNK), half), v), state
    )


def aligned(first):
    return pl.ds(pl.multiple_of(first, 16), PART)


def load_queries(qd, qbuf, qgrp, q_group, q_live, q_first):
    qbuf[...] = jnp.zeros_like(qbuf)
    row = lax.broadcasted_iota(jnp.int32, (PART, COLS), 0)
    lane = lax.broadcasted_iota(jnp.int32, (8, QROWS), 1)
    lane_group = jnp.full((8, QROWS), -1, jnp.int32)
    for s in range(4):
        for j in range(4):
            n = s * 4 + j
            rows = aligned(q_first[n])
            live = row < q_live[n]
            for a in range(2):
                qbuf[a, rows, :] = jnp.where(live, qd[s][j, a], qbuf[a, rows, :])
            here = (lane >= q_first[n]) & (lane < q_first[n] + q_live[n])
            lane_group = jnp.where(here, q_group[n], lane_group)
    qgrp[...] = lane_group


def load_keys(kv, kbuf, kgrp, k_group, k_live, k_first):
    kbuf[...] = jnp.zeros_like(kbuf)
    kgrp[...] = jnp.full_like(kgrp, FAR)
    row = lax.broadcasted_iota(jnp.int32, (PART, COLS), 0)
    row_lanes = lax.broadcasted_iota(jnp.int32, (PART, HD), 0)
    for j in range(4):
        for s in range(4):
            rows = aligned(k_first[j][s])
            live = row < k_live[j][s]
            for a in range(2):
                kbuf[a, rows, :] = jnp.where(live, kv[s][j, a], kbuf[a, rows, :])
            kgrp[rows, :] = jnp.where(row_lanes < k_live[j][s], k_group[j], kgrp[rows, :])


def stats_kernel(o, table, *refs):
    q_group, q_live, q_first = read_queries(table)
    k_group, k_live, k_first, blocks = read_keys(table, o)
    if o == 0:
        qbuf, qgrp, kbuf, kgrp, stats = refs[6:11]
        load_queries(pieces(*refs[0:3]), qbuf, qgrp, q_group, q_live, q_first)
    else:
        qbuf, qgrp, before = refs[0:3]
        kbuf, kgrp, stats = refs[6:9]
    load_keys(pieces(*refs[3:6]), kbuf, kgrp, k_group, k_live, k_first)
    stats[...] = jnp.zeros_like(stats)
    def chunk(n, _):
        rows = pl.ds(pl.multiple_of(n * QCHUNK, QCHUNK), QCHUNK)

        def step(keys, carry):
            group = kgrp[keys, :]
            ok = jnp.concatenate([group] * (QCHUNK // HD), axis=1) <= qgrp[0:1, rows]
            out = []
            for h in range(HEADS):
                cols = slice(h * HD, (h + 1) * HD)
                top, total, weighted = carry[h]
                scores = dot(kbuf[0, keys, cols], qbuf[0, rows, cols], NT)
                dprobs = dot(kbuf[1, keys, cols], qbuf[1, rows, cols], NT)
                scores = jnp.where(ok, scores * (SCALE * LOG2E), NEG)
                new_top = jnp.maximum(top, jnp.max(scores, axis=0, keepdims=True))
                weights = jnp.exp2(scores - new_top)
                factor = jnp.exp2(top - new_top)
                total = total * factor + jnp.sum(weights, axis=0, keepdims=True)
                weighted = weighted * factor + jnp.sum(weights * dprobs, axis=0, keepdims=True)
                out.append((new_top, total, weighted))
            return tuple(out)

        if o == 0:
            start = (
                jnp.full((1, QCHUNK), LOW, jnp.float32),
                jnp.zeros((1, QCHUNK), jnp.float32),
                jnp.zeros((1, QCHUNK), jnp.float32),
            )
            start = (start,) * HEADS
        else:
            start = tuple(
                tuple(before[3 * k + h : 3 * k + h + 1, rows] for k in range(3)) for h in range(HEADS)
            )
        final = visit(pick(blocks, n), step, start)
        for h in range(HEADS):
            for k in range(3):
                stats[3 * k + h : 3 * k + h + 1, rows] = final[h][k]
        return 0

    lax.fori_loop(0, QROWS // QCHUNK, chunk, 0)


def combine(parts, levels):
    sts = [st[...] for st in parts]
    top = functools.reduce(jnp.maximum, [st[0:3, :] for st in sts])
    factors = [jnp.exp2(st[0:3, :] - top) for st in sts]
    total = sum(f * st[3:6, :] for f, st in zip(factors, sts))
    weighted = sum(f * st[6:9, :] for f, st in zip(factors, sts))
    some = total > 0.0
    safe = jnp.where(some, total, 1.0)
    levels[0:3, :] = jnp.where(some, top + jnp.log2(safe), 0.0)
    levels[3:6, :] = weighted / safe
    levels[6:8, :] = jnp.zeros_like(levels[6:8, :])


def grad_kernel(o, table, qbuf, qgrp, kbuf, kgrp, *refs):
    q_group, q_live, q_first = read_queries(table)
    k_group, k_live, k_first, blocks = read_keys(table, o)
    if o == 1:
        dkv, dqt, levels, dks, dvs = refs[4:9]
        combine(refs[0:4], levels)
        dqt[...] = jnp.zeros_like(dqt)
    else:
        before, levels, dkv, dq, dqt, dks, dvs, dqs = refs
        dqt[...] = before[...]
    dks[...] = jnp.zeros_like(dks)
    dvs[...] = jnp.zeros_like(dvs)

    def chunk(n, _):
        rows = pl.ds(pl.multiple_of(n * QCHUNK, QCHUNK), QCHUNK)

        def step(keys, _):
            group = kgrp[keys, :]
            ok = jnp.concatenate([group] * (QCHUNK // HD), axis=1) <= qgrp[0:1, rows]
            products = []
            for h in range(HEADS):
                cols = slice(h * HD, (h + 1) * HD)
                scores = dot(kbuf[0, keys, cols], qbuf[0, rows, cols], NT)
                products.append((scores, dot(kbuf[1, keys, cols], qbuf[1, rows, cols], NT)))
            weights = []
            for h in range(HEADS):
                scores, dprobs = products[h]
                scores = jnp.where(ok, scores * (SCALE * LOG2E), NEG)
                probs = jnp.exp2(scores - levels[h : h + 1, rows])
                dscores = probs * (dprobs - levels[3 + h : 4 + h, rows])
                weights.append((probs.astype(jnp.bfloat16), dscores.astype(jnp.bfloat16)))
            for h in range(HEADS):
                cols = slice(h * HD, (h + 1) * HD)
                probs, dscores = weights[h]
                dvs[keys, cols] += dot(probs, qbuf[1, rows, cols], NN)
                dks[keys, cols] += dot(dscores, qbuf[0, rows, cols], NN)
                dqt[h, :, rows] += dot(kbuf[0, keys, cols], dscores, TN)
            return 0

        visit(pick(blocks, n), step, 0)
        return 0

    lax.fori_loop(0, QROWS // QCHUNK, chunk, 0)
    row = lax.broadcasted_iota(jnp.int32, (PART, COLS), 0)
    for j in range(4):
        for s in range(4):
            rows = aligned(k_first[j][s])
            live = row < k_live[j][s]
            dkv[s, j, 0] = jnp.where(live, dks[rows, :] * SCALE, 0.0).astype(jnp.bfloat16)
            dkv[s, j, 1] = jnp.where(live, dvs[rows, :], 0.0).astype(jnp.bfloat16)
    if o == 0:
        for h in range(HEADS):
            dqs[:, h * HD : (h + 1) * HD] = (dqt[h] * SCALE).T
        for s in range(4):
            for j in range(4):
                n = s * 4 + j
                rows = aligned(q_first[n])
                dq[s, j] = jnp.where(row < q_live[n], dqs[rows, :], 0.0).astype(jnp.bfloat16)


SMEM = pl.BlockSpec(memory_space=pltpu.SMEM)
VMEM = pl.BlockSpec(memory_space=pltpu.VMEM)
PARAMS = pltpu.CompilerParams(vmem_limit_bytes=24 * 1024 * 1024)
LARGE = pltpu.CompilerParams(vmem_limit_bytes=60 * 1024 * 1024)
SMALL = pltpu.CompilerParams(vmem_limit_bytes=6 * 1024 * 1024)


def run(kernel, name, out_shape, tables, arrays, scratch=()):
    return pl.pallas_call(
        kernel,
        out_shape=out_shape,
        in_specs=[SMEM] * len(tables) + [VMEM] * len(arrays),
        out_specs=(VMEM,) * len(out_shape),
        scratch_shapes=list(scratch),
        compiler_params=PARAMS,
        cost_estimate=pl.CostEstimate(flops=3 * 10**9, bytes_accessed=6 * 10**6, transcendentals=2 * 10**6),
        name=name,
    )(*tables, *arrays)


def local(query, keys, values, dout, slot_group, valid):
    c = lax.axis_index("head") % NC
    bf16, f32 = jnp.bfloat16, jnp.float32

    keep, give = pl.pallas_call(
        pack_kernel,
        out_shape=(jax.ShapeDtypeStruct((4, 4, SUB, COLS), bf16),) * 2,
        in_specs=[pl.BlockSpec(memory_space=pltpu.HBM)] * 4,
        out_specs=(VMEM,) * 2,
        scratch_shapes=[pltpu.VMEM((4, SUB, NZ * COLS), bf16), pltpu.SemaphoreType.DMA((4,))],
        compiler_params=LARGE,
        name="pack",
    )(query, dout, keys, values)
    take = swap_core(give)
    both = jnp.where(c == 0, jnp.concatenate([keep, take], axis=2), jnp.concatenate([take, keep], axis=2))
    i32 = jnp.int32
    slot_group, valid, both = lax.optimization_barrier((slot_group, valid, both))
    table = pl.pallas_call(
        table_kernel,
        out_shape=jax.ShapeDtypeStruct((128,), i32),
        in_specs=[SMEM] * 2,
        out_specs=SMEM,
        compiler_params=SMALL,
        cost_estimate=pl.CostEstimate(flops=2 * 10**9, bytes_accessed=10**6, transcendentals=0),
        name="table",
    )(slot_group, valid)
    got = {j: send(both[j], lambda y, z, x, c: (y, z + c + 2 * j, x, c)) for j in (2, 1, 3, 0)}
    own_qd = jnp.stack([got[j][0:2] for j in range(4)])
    own_kv = jnp.stack([got[j][2:4] for j in range(4)])

    kv_first, qd_first, table = lax.optimization_barrier((first_x(own_kv), first_y(own_qd), table))
    tables = (table,)
    kv_rest = second_x(jnp.stack([own_kv, kv_first]))
    qd_rest = second_y(jnp.stack([own_qd, qd_first]))

    kbuf_type = jax.ShapeDtypeStruct((2, KROWS, COLS), bf16)
    kgrp_type = jax.ShapeDtypeStruct((KROWS, HD), i32)
    stats_type = jax.ShapeDtypeStruct((16, QROWS), f32)
    qbuf, qgrp, kbuf, kgrp, part = run(
        functools.partial(stats_kernel, 0),
        "stats_own",
        (jax.ShapeDtypeStruct((2, QROWS, COLS), bf16), jax.ShapeDtypeStruct((8, QROWS), i32))
        + (kbuf_type, kgrp_type, stats_type),
        tables,
        (own_qd, qd_first, qd_rest, own_kv, kv_first, kv_rest),
    )
    kbuf_other, kgrp_other, stats = run(
        functools.partial(stats_kernel, 1),
        "stats_other",
        (kbuf_type, kgrp_type, stats_type),
        tables,
        (qbuf, qgrp, part, swap_core(own_kv), swap_core(kv_first), swap_core(kv_rest)),
    )

    all_stats = [stats] + [send(stats, lambda y, z, x, c: (y + n, z, x, c)) for n in (1, 2, 3)]

    dkv_type = jax.ShapeDtypeStruct((4, 4, 2, PART, COLS), bf16)
    scratch = [
        pltpu.VMEM((HEADS, HD, QROWS), f32),
        pltpu.VMEM((KROWS, COLS), f32),
        pltpu.VMEM((KROWS, COLS), f32),
    ]
    dkv_other, dqt, levels = run(
        functools.partial(grad_kernel, 1),
        "grads_other",
        (
            dkv_type,
            jax.ShapeDtypeStruct((HEADS, HD, QROWS), f32),
            jax.ShapeDtypeStruct((8, QROWS), f32),
        ),
        tables,
        (qbuf, qgrp, kbuf_other, kgrp_other, *all_stats),
        scratch[1:],
    )
    swapped = swap_core(dkv_other)
    dkv_own, dq = run(
        functools.partial(grad_kernel, 0),
        "grads_own",
        (dkv_type, jax.ShapeDtypeStruct((4, 4, PART, COLS), bf16)),
        tables,
        (qbuf, qgrp, kbuf, kgrp, dqt, levels),
        scratch + [pltpu.VMEM((QROWS, COLS), f32)],
    )

    dkv_sum = dkv_own.astype(f32) + swapped.astype(f32)
    dkv_half, dq_half = lax.optimization_barrier((second_x(dkv_sum[2:4].astype(bf16)), second_y(dq[2:4])))
    dkv_sum = dkv_sum[0:2] + dkv_half.astype(f32)
    dq_sum = dq[0:2].astype(f32) + dq_half.astype(f32)
    dkv_last, dq_last = lax.optimization_barrier(
        (first_x(dkv_sum[1].astype(bf16)), first_y(dq_sum[1].astype(bf16)))
    )
    dkv_sum = (dkv_sum[0] + dkv_last.astype(f32)).astype(bf16)
    dq_sum = (dq_sum[0] + dq_last.astype(f32)).astype(bf16)

    back = {}
    for j in (2, 1, 3, 0):
        block = jnp.concatenate([dq_sum[j][None], dkv_sum[j]], axis=0)
        back[j] = send(block, lambda y, z, x, c: (y, z - c - 2 * j, x, c))
    back = [back[j] for j in range(4)]
    first = jnp.stack([b[:, :SUB] for b in back])
    second = jnp.stack([b[:, SUB:] for b in back])
    theirs = swap_core(jnp.where(c == 0, second, first))
    return pl.pallas_call(
        unpack_kernel,
        out_shape=(jax.ShapeDtypeStruct((SUB, NZ * COLS), bf16),) * 3,
        in_specs=[VMEM] * 2,
        out_specs=(VMEM,) * 3,
        compiler_params=SMALL,
        name="unpack",
    )(jnp.where(c == 0, first, second), theirs)


def solution(mesh):
    spec = P(("tm", "head"), None)
    return jax.shard_map(
        local,
        mesh=mesh,
        in_specs=(spec, spec, spec, spec, P(), P()),
        out_specs=(spec, spec, spec),
        check_vma=False,
    )
```

```python
import functools
import math

import jax
import jax.numpy as jnp
from jax import lax
from jax.experimental import pallas as pl
from jax.experimental.pallas import tpu as pltpu
from jax.sharding import PartitionSpec as P

HD = 128
HEADS = 3
COLS = HEADS * HD
NY, NZ, NX, NC = 4, 8, 4, 2
PART = 48
SUB = 24
QROWS = 768
NEG = -1e30
LOW = -1e29
FAR = 1000
SCALE = 1.0 / math.sqrt(HD)
LOG2E = 1.4426950408889634
QCHUNK = 256
LANE_BLOCKS = QROWS // HD
LEVEL_ROWS = 24
KROWS = 768
KCHUNK = 512

NT = (((1,), (1,)), ((), ()))
NN = (((1,), (0,)), ((), ()))
TN = (((0,), (0,)), ((), ()))


def pairs(move):
    out = []
    for y in range(NY):
        for z in range(NZ):
            for x in range(NX):
                for c in range(NC):
                    ty, tz, tx, tc = move(y, z, x, c)
                    ty, tz, tx = ty % NY, tz % NZ, tx % NX
                    out.append((((y * NZ + z) * NX + x) * NC + c, ((ty * NZ + tz) * NX + tx) * NC + tc))
    return out


def send(array, move):
    return lax.ppermute(array, ("tm", "head"), pairs(move))


def swap_core(array):
    return send(array, lambda y, z, x, c: (y, z, x, 1 - c))


def dot(a, b, dims):
    return lax.dot_general(a, b, dims, preferred_element_type=jnp.float32)


def position():
    tm = lax.axis_index("tm")
    head = lax.axis_index("head")
    return tm // NZ, tm % NZ, head // NC, head % NC


def pack_kernel(query, grad, keys, values, keep, give, rows, sems):
    _, z, _, c = position()
    copies = [
        pltpu.make_async_copy(array, rows.at[n], sems.at[n])
        for n, array in enumerate((query, grad, keys, values))
    ]
    for copy in copies:
        copy.start()
    for copy in copies:
        copy.wait()
    for j in range(4):
        mine = pl.ds(pl.multiple_of(((z + c + 2 * j) & 7) * COLS, HD), COLS)
        theirs = pl.ds(pl.multiple_of(((z + 1 - c + 2 * j) & 7) * COLS, HD), COLS)
        for n in range(4):
            keep[j, n] = rows[n, :, mine]
            give[j, n] = rows[n, :, theirs]


def unpack_kernel(mine, theirs, *outs):
    _, z, _, c = position()
    for j in range(4):
        own = pl.ds(pl.multiple_of(((z + c + 2 * j) & 7) * COLS, HD), COLS)
        other = pl.ds(pl.multiple_of(((z + 1 - c + 2 * j) & 7) * COLS, HD), COLS)
        for n in range(3):
            outs[n][:, own] = mine[j, n]
            outs[n][:, other] = theirs[j, n]


def flip(s, core):
    return (0, 1 + 2 * core, 3 - 2 * core, 2)[s]


def query_slot(at, s, j):
    return (at[0] ^ flip(s, at[3])) * NZ + ((at[1] - at[3] - 2 * j) & 7)


def key_slot(at, o, j):
    core = 1 - at[3] if o else at[3]
    return at[0] * NZ + ((at[1] - core - 2 * j) & 7)


def key_part(at, o, s):
    return at[2] ^ flip(s, 1 - at[3] if o else at[3])


def first_y(array):
    return send(array, lambda y, z, x, c: (y ^ (1 + 2 * c), z, x, c))


def second_y(array):
    return send(array, lambda y, z, x, c: (y ^ (3 - 2 * c), z, x, c))


def first_x(array):
    return send(array, lambda y, z, x, c: (y, z, x ^ (1 + 2 * c), c))


def second_x(array):
    return send(array, lambda y, z, x, c: (y, z, x ^ (3 - 2 * c), c))


def pieces(pair, rest):
    return (pair.at[0], pair.at[1], rest.at[0], rest.at[1])


def lanes(ref, first, n):
    blocks = QCHUNK // HD
    return jnp.concatenate([ref[pl.ds(first + blocks * n + i, 1), :] for i in range(blocks)], axis=1)


def clip_rows(count):
    return jnp.minimum(jnp.maximum(count, 0), PART)


def round_rows(count):
    return ((count + 15) // 16) * 16


def place_queries(at, groups, valid):
    group = [groups[query_slot(at, s, j)] for s in range(4) for j in range(4)]
    live = [clip_rows(valid[g] - PART * at[2]) for g in group]
    padded = [round_rows(n) for n in live]
    first = [sum(jnp.where(other < mine, n, 0) for other, n in zip(group, padded)) for mine in group]
    tops = []
    for n in range(QROWS // QCHUNK):
        inside = [
            jnp.where((f < QCHUNK * (n + 1)) & (count > 0), g, -1) for g, f, count in zip(group, first, live)
        ]
        tops.append(jnp.where(sum(padded) > QCHUNK * n, functools.reduce(jnp.maximum, inside), -1))
    return group, live, first, tops


def place_keys(at, groups, valid, o, tops):
    group = [groups[key_slot(at, o, j)] for j in range(4)]
    rows = [round_rows(valid[g]) for g in group]
    first, live = [], []
    for mine in group:
        here = sum(jnp.where(other < mine, n, 0) for other, n in zip(group, rows))
        firsts, lives = [], []
        for s in range(4):
            count = clip_rows(valid[mine] - PART * key_part(at, o, s))
            firsts.append(here)
            lives.append(count)
            here = here + round_rows(count)
        first.append(firsts)
        live.append(lives)
    half = KCHUNK // 2
    blocks = []
    for top in tops:
        seen = sum(jnp.where(g <= top, n, 0) for g, n in zip(group, rows))
        blocks.append((seen + half - 1) // half)
    return group, live, first, blocks


def table_kernel(groups, valid, table):
    at = position()
    q_group, q_live, q_first, tops = place_queries(at, groups, valid)
    for n in range(16):
        table[n] = q_group[n]
        table[16 + n] = q_live[n]
        table[32 + n] = q_first[n]
    for o in range(2):
        k_group, k_live, k_first, blocks = place_keys(at, groups, valid, o, tops)
        for j in range(4):
            table[48 + 4 * o + j] = k_group[j]
            for s in range(4):
                table[56 + 16 * o + 4 * j + s] = k_live[j][s]
                table[88 + 16 * o + 4 * j + s] = k_first[j][s]
        for n in range(QROWS // QCHUNK):
            table[120 + 3 * o + n] = blocks[n]
    table[126] = 0
    table[127] = 0


def read_queries(table):
    return tuple([table[first + n] for n in range(16)] for first in (0, 16, 32))


def read_keys(table, o):
    group = [table[48 + 4 * o + j] for j in range(4)]
    live = [[table[56 + 16 * o + 4 * j + s] for s in range(4)] for j in range(4)]
    first = [[table[88 + 16 * o + 4 * j + s] for s in range(4)] for j in range(4)]
    return group, live, first, [table[120 + 3 * o + n] for n in range(QROWS // QCHUNK)]


def pick(values, n):
    out = values[-1]
    for i in range(len(values) - 1):
        out = jnp.where(n == i, values[i], out)
    return out


def visit(blocks, step, state):
    half = KCHUNK // 2
    whole = blocks // 2
    state = lax.fori_loop(0, whole, lambda i, v: step(pl.ds(pl.multiple_of(i * KCHUNK, KCHUNK), KCHUNK), v), state)
    return lax.fori_loop(
        0, blocks - 2 * whole, lambda i, v: step(pl.ds(pl.multiple_of(whole * KCHUNK, KCHUNK), half), v), state
    )


def aligned(first):
    return pl.ds(pl.multiple_of(first, 16), PART)


def load_queries(qd, qbuf, qgrp, q_group, q_live, q_first):
    qbuf[...] = jnp.zeros_like(qbuf)
    row = lax.broadcasted_iota(jnp.int32, (PART, COLS), 0)
    lane = lax.broadcasted_iota(jnp.int32, (8, QROWS), 1)
    lane_group = jnp.full((8, QROWS), -1, jnp.int32)
    for s in range(4):
        for j in range(4):
            n = s * 4 + j
            rows = aligned(q_first[n])
            live = row < q_live[n]
            for a in range(2):
                qbuf[a, rows, :] = jnp.where(live, qd[s][j, a], qbuf[a, rows, :])
            here = (lane >= q_first[n]) & (lane < q_first[n] + q_live[n])
            lane_group = jnp.where(here, q_group[n], lane_group)
    qgrp[...] = lane_group


def load_keys(kv, kbuf, kgrp, k_group, k_live, k_first):
    kbuf[...] = jnp.zeros_like(kbuf)
    kgrp[...] = jnp.full_like(kgrp, FAR)
    row = lax.broadcasted_iota(jnp.int32, (PART, COLS), 0)
    row_lanes = lax.broadcasted_iota(jnp.int32, (PART, HD), 0)
    for j in range(4):
        for s in range(4):
            rows = aligned(k_first[j][s])
            live = row < k_live[j][s]
            for a in range(2):
                kbuf[a, rows, :] = jnp.where(live, kv[s][j, a], kbuf[a, rows, :])
            kgrp[rows, :] = jnp.where(row_lanes < k_live[j][s], k_group[j], kgrp[rows, :])


def stats_kernel(o, table, *refs):
    q_group, q_live, q_first = read_queries(table)
    k_group, k_live, k_first, blocks = read_keys(table, o)
    if o == 0:
        qbuf, qgrp, kbuf, kgrp, stats = refs[4:9]
        load_queries(pieces(*refs[0:2]), qbuf, qgrp, q_group, q_live, q_first)
    else:
        qbuf, qgrp, before = refs[0:3]
        kbuf, kgrp, stats = refs[5:8]
    load_keys(pieces(*refs[2 + o : 4 + o]), kbuf, kgrp, k_group, k_live, k_first)
    stats[...] = jnp.zeros_like(stats)
    def chunk(n, _):
        rows = pl.ds(pl.multiple_of(n * QCHUNK, QCHUNK), QCHUNK)

        def step(keys, carry):
            group = kgrp[keys, :]
            ok = jnp.concatenate([group] * (QCHUNK // HD), axis=1) <= qgrp[0:1, rows]
            out = []
            for h in range(HEADS):
                cols = slice(h * HD, (h + 1) * HD)
                top, total, weighted = carry[h]
                scores = dot(kbuf[0, keys, cols], qbuf[0, rows, cols], NT)
                dprobs = dot(kbuf[1, keys, cols], qbuf[1, rows, cols], NT)
                scores = jnp.where(ok, scores * (SCALE * LOG2E), NEG)
                new_top = jnp.maximum(top, jnp.max(scores, axis=0, keepdims=True))
                weights = jnp.exp2(scores - new_top)
                factor = jnp.exp2(top - new_top)
                total = total * factor + jnp.sum(weights, axis=0, keepdims=True)
                weighted = weighted * factor + jnp.sum(weights * dprobs, axis=0, keepdims=True)
                out.append((new_top, total, weighted))
            return tuple(out)

        if o == 0:
            start = (
                jnp.full((1, QCHUNK), LOW, jnp.float32),
                jnp.zeros((1, QCHUNK), jnp.float32),
                jnp.zeros((1, QCHUNK), jnp.float32),
            )
            start = (start,) * HEADS
        else:
            start = tuple(
                tuple(lanes(before, (3 * k + h) * LANE_BLOCKS, n) for k in range(3)) for h in range(HEADS)
            )
        final = visit(pick(blocks, n), step, start)
        for h in range(HEADS):
            for k in range(3):
                for i in range(QCHUNK // HD):
                    place = pl.ds((3 * k + h) * LANE_BLOCKS + n * (QCHUNK // HD) + i, 1)
                    stats[place, :] = final[h][k][:, i * HD : (i + 1) * HD]
        return 0

    lax.fori_loop(0, QROWS // QCHUNK, chunk, 0)


def combine(parts, levels):
    sts = [st[...] for st in parts]
    size = HEADS * LANE_BLOCKS
    top = functools.reduce(jnp.maximum, [st[0:size] for st in sts])
    factors = [jnp.exp2(st[0:size] - top) for st in sts]
    total = sum(f * st[size : 2 * size] for f, st in zip(factors, sts))
    weighted = sum(f * st[2 * size : 3 * size] for f, st in zip(factors, sts))
    some = total > 0.0
    safe = jnp.where(some, total, 1.0)
    levels[...] = jnp.zeros_like(levels)
    levels[0:size, :] = jnp.where(some, top + jnp.log2(safe), 0.0)
    levels[LEVEL_ROWS : LEVEL_ROWS + size, :] = weighted / safe


def grad_kernel(o, table, qbuf, qgrp, kbuf, kgrp, *refs):
    q_group, q_live, q_first = read_queries(table)
    k_group, k_live, k_first, blocks = read_keys(table, o)
    if o == 1:
        dkv, dqt, levels, dks, dvs = refs[4:9]
        combine(refs[0:4], levels)
        dqt[...] = jnp.zeros_like(dqt)
    else:
        before, levels, dkv, dq, dqt, dks, dvs, dqs = refs
        dqt[...] = before[...]
    dks[...] = jnp.zeros_like(dks)
    dvs[...] = jnp.zeros_like(dvs)

    def chunk(n, _):
        rows = pl.ds(pl.multiple_of(n * QCHUNK, QCHUNK), QCHUNK)

        def step(keys, _):
            group = kgrp[keys, :]
            ok = jnp.concatenate([group] * (QCHUNK // HD), axis=1) <= qgrp[0:1, rows]
            products = []
            for h in range(HEADS):
                cols = slice(h * HD, (h + 1) * HD)
                scores = dot(kbuf[0, keys, cols], qbuf[0, rows, cols], NT)
                products.append((scores, dot(kbuf[1, keys, cols], qbuf[1, rows, cols], NT)))
            weights = []
            for h in range(HEADS):
                scores, dprobs = products[h]
                scores = jnp.where(ok, scores * (SCALE * LOG2E), NEG)
                probs = jnp.exp2(scores - lanes(levels, h * LANE_BLOCKS, n))
                dscores = probs * (dprobs - lanes(levels, LEVEL_ROWS + h * LANE_BLOCKS, n))
                weights.append((probs.astype(jnp.bfloat16), dscores.astype(jnp.bfloat16)))
            for h in range(HEADS):
                cols = slice(h * HD, (h + 1) * HD)
                probs, dscores = weights[h]
                dvs[keys, cols] += dot(probs, qbuf[1, rows, cols], NN)
                dks[keys, cols] += dot(dscores, qbuf[0, rows, cols], NN)
                dqt[h, :, rows] += dot(kbuf[0, keys, cols], dscores, TN)
            return 0

        visit(pick(blocks, n), step, 0)
        return 0

    lax.fori_loop(0, QROWS // QCHUNK, chunk, 0)
    row = lax.broadcasted_iota(jnp.int32, (PART, COLS), 0)
    for j in range(4):
        for s in range(4):
            rows = aligned(k_first[j][s])
            live = row < k_live[j][s]
            dkv[s, j, 0] = jnp.where(live, dks[rows, :] * SCALE, 0.0).astype(jnp.bfloat16)
            dkv[s, j, 1] = jnp.where(live, dvs[rows, :], 0.0).astype(jnp.bfloat16)
    if o == 0:
        for h in range(HEADS):
            dqs[:, h * HD : (h + 1) * HD] = (dqt[h] * SCALE).T
        for s in range(4):
            for j in range(4):
                n = s * 4 + j
                rows = aligned(q_first[n])
                dq[s, j] = jnp.where(row < q_live[n], dqs[rows, :], 0.0).astype(jnp.bfloat16)


SMEM = pl.BlockSpec(memory_space=pltpu.SMEM)
VMEM = pl.BlockSpec(memory_space=pltpu.VMEM)
PARAMS = pltpu.CompilerParams(vmem_limit_bytes=24 * 1024 * 1024)
LARGE = pltpu.CompilerParams(vmem_limit_bytes=60 * 1024 * 1024)
SMALL = pltpu.CompilerParams(vmem_limit_bytes=6 * 1024 * 1024)


def run(kernel, name, out_shape, tables, arrays, scratch=()):
    return pl.pallas_call(
        kernel,
        out_shape=out_shape,
        in_specs=[SMEM] * len(tables) + [VMEM] * len(arrays),
        out_specs=(VMEM,) * len(out_shape),
        scratch_shapes=list(scratch),
        compiler_params=PARAMS,
        cost_estimate=pl.CostEstimate(flops=3 * 10**9, bytes_accessed=6 * 10**6, transcendentals=2 * 10**6),
        name=name,
    )(*tables, *arrays)


def local(query, keys, values, dout, slot_group, valid):
    c = lax.axis_index("head") % NC
    bf16, f32 = jnp.bfloat16, jnp.float32

    keep, give = pl.pallas_call(
        pack_kernel,
        out_shape=(jax.ShapeDtypeStruct((4, 4, SUB, COLS), bf16),) * 2,
        in_specs=[pl.BlockSpec(memory_space=pltpu.HBM)] * 4,
        out_specs=(VMEM,) * 2,
        scratch_shapes=[pltpu.VMEM((4, SUB, NZ * COLS), bf16), pltpu.SemaphoreType.DMA((4,))],
        compiler_params=LARGE,
        name="pack",
    )(query, dout, keys, values)
    take = swap_core(give)
    both = jnp.where(c == 0, jnp.concatenate([keep, take], axis=2), jnp.concatenate([take, keep], axis=2))
    i32 = jnp.int32
    slot_group, valid, both = lax.optimization_barrier((slot_group, valid, both))
    table = pl.pallas_call(
        table_kernel,
        out_shape=jax.ShapeDtypeStruct((128,), i32),
        in_specs=[SMEM] * 2,
        out_specs=SMEM,
        compiler_params=SMALL,
        cost_estimate=pl.CostEstimate(flops=2 * 10**9, bytes_accessed=10**6, transcendentals=0),
        name="table",
    )(slot_group, valid)
    got = {j: send(both[j], lambda y, z, x, c: (y, z + c + 2 * j, x, c)) for j in (2, 1, 3, 0)}
    own_qd = jnp.stack([got[j][0:2] for j in range(4)])
    own_kv = jnp.stack([got[j][2:4] for j in range(4)])

    kv_first, qd_first, table = lax.optimization_barrier((first_x(own_kv), first_y(own_qd), table))
    tables = (table,)
    kv_pair = jnp.stack([own_kv, kv_first])
    qd_pair = jnp.stack([own_qd, qd_first])
    kv_rest = second_x(kv_pair)
    qd_rest = second_y(qd_pair)

    kbuf_type = jax.ShapeDtypeStruct((2, KROWS, COLS), bf16)
    kgrp_type = jax.ShapeDtypeStruct((KROWS, HD), i32)
    stats_type = jax.ShapeDtypeStruct((56, HD), f32)
    qbuf, qgrp, kbuf, kgrp, part = run(
        functools.partial(stats_kernel, 0),
        "stats_own",
        (jax.ShapeDtypeStruct((2, QROWS, COLS), bf16), jax.ShapeDtypeStruct((8, QROWS), i32))
        + (kbuf_type, kgrp_type, stats_type),
        tables,
        (qd_pair, qd_rest, kv_pair, kv_rest),
    )
    kbuf_other, kgrp_other, stats = run(
        functools.partial(stats_kernel, 1),
        "stats_other",
        (kbuf_type, kgrp_type, stats_type),
        tables,
        (qbuf, qgrp, part, swap_core(kv_pair), swap_core(kv_rest)),
    )

    all_stats = [stats] + [send(stats, lambda y, z, x, c: (y + n, z, x, c)) for n in (1, 2, 3)]

    dkv_type = jax.ShapeDtypeStruct((4, 4, 2, PART, COLS), bf16)
    scratch = [
        pltpu.VMEM((HEADS, HD, QROWS), f32),
        pltpu.VMEM((KROWS, COLS), f32),
        pltpu.VMEM((KROWS, COLS), f32),
    ]
    dkv_other, dqt, levels = run(
        functools.partial(grad_kernel, 1),
        "grads_other",
        (
            dkv_type,
            jax.ShapeDtypeStruct((HEADS, HD, QROWS), f32),
            jax.ShapeDtypeStruct((2 * LEVEL_ROWS, HD), f32),
        ),
        tables,
        (qbuf, qgrp, kbuf_other, kgrp_other, *all_stats),
        scratch[1:],
    )
    swapped = swap_core(dkv_other)
    dkv_own, dq = run(
        functools.partial(grad_kernel, 0),
        "grads_own",
        (dkv_type, jax.ShapeDtypeStruct((4, 4, PART, COLS), bf16)),
        tables,
        (qbuf, qgrp, kbuf, kgrp, dqt, levels),
        scratch + [pltpu.VMEM((QROWS, COLS), f32)],
    )

    dkv_sum = dkv_own.astype(f32) + swapped.astype(f32)
    dkv_half, dq_half = lax.optimization_barrier((second_x(dkv_sum[2:4].astype(bf16)), second_y(dq[2:4])))
    dkv_sum = dkv_sum[0:2] + dkv_half.astype(f32)
    dq_sum = dq[0:2].astype(f32) + dq_half.astype(f32)
    dkv_last, dq_last = lax.optimization_barrier(
        (first_x(dkv_sum[1].astype(bf16)), first_y(dq_sum[1].astype(bf16)))
    )
    dkv_sum = (dkv_sum[0] + dkv_last.astype(f32)).astype(bf16)
    dq_sum = (dq_sum[0] + dq_last.astype(f32)).astype(bf16)

    back = {}
    for j in (2, 1, 3, 0):
        block = jnp.concatenate([dq_sum[j][None], dkv_sum[j]], axis=0)
        back[j] = send(block, lambda y, z, x, c: (y, z - c - 2 * j, x, c))
    back = [back[j] for j in range(4)]
    first = jnp.stack([b[:, :SUB] for b in back])
    second = jnp.stack([b[:, SUB:] for b in back])
    theirs = swap_core(jnp.where(c == 0, second, first))
    return pl.pallas_call(
        unpack_kernel,
        out_shape=(jax.ShapeDtypeStruct((SUB, NZ * COLS), bf16),) * 3,
        in_specs=[VMEM] * 2,
        out_specs=(VMEM,) * 3,
        compiler_params=SMALL,
        name="unpack",
    )(jnp.where(c == 0, first, second), theirs)


def solution(mesh):
    spec = P(("tm", "head"), None)
    return jax.shard_map(
        local,
        mesh=mesh,
        in_specs=(spec, spec, spec, spec, P(), P()),
        out_specs=(spec, spec, spec),
        check_vma=False,
    )
```

```python
import functools
import math

import jax
import jax.numpy as jnp
from jax import lax
from jax.experimental import pallas as pl
from jax.experimental.pallas import tpu as pltpu
from jax.sharding import PartitionSpec as P

HD = 128
HEADS = 3
COLS = HEADS * HD
NY, NZ, NX, NC = 4, 8, 4, 2
PART = 48
SUB = 24
QROWS = 768
NEG = -1e30
LOW = -1e29
FAR = 1000
SCALE = 1.0 / math.sqrt(HD)
LOG2E = 1.4426950408889634
QCHUNK = 256
KROWS = 768
KCHUNK = 512

NT = (((1,), (1,)), ((), ()))
NN = (((1,), (0,)), ((), ()))
TN = (((0,), (0,)), ((), ()))


def pairs(move):
    out = []
    for y in range(NY):
        for z in range(NZ):
            for x in range(NX):
                for c in range(NC):
                    ty, tz, tx, tc = move(y, z, x, c)
                    ty, tz, tx = ty % NY, tz % NZ, tx % NX
                    out.append((((y * NZ + z) * NX + x) * NC + c, ((ty * NZ + tz) * NX + tx) * NC + tc))
    return out


def send(array, move):
    return lax.ppermute(array, ("tm", "head"), pairs(move))


def swap_core(array):
    return send(array, lambda y, z, x, c: (y, z, x, 1 - c))


def dot(a, b, dims):
    return lax.dot_general(a, b, dims, preferred_element_type=jnp.float32)


def position():
    tm = lax.axis_index("tm")
    head = lax.axis_index("head")
    return tm // NZ, tm % NZ, head // NC, head % NC


def pack_kernel(query, grad, keys, values, keep, give, rows, sems):
    _, z, _, c = position()
    copies = [
        pltpu.make_async_copy(array, rows.at[n], sems.at[n])
        for n, array in enumerate((query, grad, keys, values))
    ]
    for copy in copies:
        copy.start()
    for copy in copies:
        copy.wait()
    for j in range(4):
        mine = pl.ds(pl.multiple_of(((z + c + 2 * j) & 7) * COLS, HD), COLS)
        theirs = pl.ds(pl.multiple_of(((z + 1 - c + 2 * j) & 7) * COLS, HD), COLS)
        for n in range(4):
            keep[j, n] = rows[n, :, mine]
            give[j, n] = rows[n, :, theirs]


def unpack_kernel(mine, theirs, *outs):
    _, z, _, c = position()
    for j in range(4):
        own = pl.ds(pl.multiple_of(((z + c + 2 * j) & 7) * COLS, HD), COLS)
        other = pl.ds(pl.multiple_of(((z + 1 - c + 2 * j) & 7) * COLS, HD), COLS)
        for n in range(3):
            outs[n][:, own] = mine[j, n]
            outs[n][:, other] = theirs[j, n]


def flip(s, core):
    return (0, 1 + 2 * core, 3 - 2 * core, 2)[s]


def query_slot(at, s, j):
    return (at[0] ^ flip(s, at[3])) * NZ + ((at[1] - at[3] - 2 * j) & 7)


def key_slot(at, o, j):
    core = 1 - at[3] if o else at[3]
    return at[0] * NZ + ((at[1] - core - 2 * j) & 7)


def key_part(at, o, s):
    return at[2] ^ flip(s, 1 - at[3] if o else at[3])


def first_y(array):
    return send(array, lambda y, z, x, c: (y ^ (1 + 2 * c), z, x, c))


def second_y(array):
    return send(array, lambda y, z, x, c: (y ^ (3 - 2 * c), z, x, c))


def first_x(array):
    return send(array, lambda y, z, x, c: (y, z, x ^ (1 + 2 * c), c))


def second_x(array):
    return send(array, lambda y, z, x, c: (y, z, x ^ (3 - 2 * c), c))


def pieces(own, first, rest):
    return (own, first, rest.at[0], rest.at[1])


def clip_rows(count):
    return jnp.minimum(jnp.maximum(count, 0), PART)


def round_rows(count):
    return ((count + 15) // 16) * 16


def place_queries(at, groups, valid):
    group = [groups[query_slot(at, s, j)] for s in range(4) for j in range(4)]
    live = [clip_rows(valid[g] - PART * at[2]) for g in group]
    padded = [round_rows(n) for n in live]
    first = [sum(jnp.where(other < mine, n, 0) for other, n in zip(group, padded)) for mine in group]
    tops = []
    for n in range(QROWS // QCHUNK):
        inside = [
            jnp.where((f < QCHUNK * (n + 1)) & (count > 0), g, -1) for g, f, count in zip(group, first, live)
        ]
        tops.append(jnp.where(sum(padded) > QCHUNK * n, functools.reduce(jnp.maximum, inside), -1))
    return group, live, first, tops


def place_keys(at, groups, valid, o, tops):
    group = [groups[key_slot(at, o, j)] for j in range(4)]
    rows = [round_rows(valid[g]) for g in group]
    first, live = [], []
    for mine in group:
        here = sum(jnp.where(other < mine, n, 0) for other, n in zip(group, rows))
        firsts, lives = [], []
        for s in range(4):
            count = clip_rows(valid[mine] - PART * key_part(at, o, s))
            firsts.append(here)
            lives.append(count)
            here = here + round_rows(count)
        first.append(firsts)
        live.append(lives)
    half = KCHUNK // 2
    blocks = []
    for top in tops:
        seen = sum(jnp.where(g <= top, n, 0) for g, n in zip(group, rows))
        blocks.append((seen + half - 1) // half)
    return group, live, first, blocks


def table_kernel(groups, valid, table):
    at = position()
    q_group, q_live, q_first, tops = place_queries(at, groups, valid)
    for n in range(16):
        table[n] = q_group[n]
        table[16 + n] = q_live[n]
        table[32 + n] = q_first[n]
    for o in range(2):
        k_group, k_live, k_first, blocks = place_keys(at, groups, valid, o, tops)
        for j in range(4):
            table[48 + 4 * o + j] = k_group[j]
            for s in range(4):
                table[56 + 16 * o + 4 * j + s] = k_live[j][s]
                table[88 + 16 * o + 4 * j + s] = k_first[j][s]
        for n in range(QROWS // QCHUNK):
            table[120 + 3 * o + n] = blocks[n]
    table[126] = 0
    table[127] = 0


def read_queries(table):
    return tuple([table[first + n] for n in range(16)] for first in (0, 16, 32))


def read_keys(table, o):
    group = [table[48 + 4 * o + j] for j in range(4)]
    live = [[table[56 + 16 * o + 4 * j + s] for s in range(4)] for j in range(4)]
    first = [[table[88 + 16 * o + 4 * j + s] for s in range(4)] for j in range(4)]
    return group, live, first, [table[120 + 3 * o + n] for n in range(QROWS // QCHUNK)]


def pick(values, n):
    out = values[-1]
    for i in range(len(values) - 1):
        out = jnp.where(n == i, values[i], out)
    return out


def visit(blocks, step, state):
    def body(rows):
        return lambda i, v: step(pl.ds(0, rows), v)

    for count in (1, 2, 3):
        state = lax.fori_loop(0, jnp.where(blocks == count, 1, 0), body(count * KCHUNK // 2), state)
    return state


def aligned(first):
    return pl.ds(pl.multiple_of(first, 16), PART)


def load_queries(qd, qbuf, qgrp, q_group, q_live, q_first):
    qbuf[...] = jnp.zeros_like(qbuf)
    row = lax.broadcasted_iota(jnp.int32, (PART, COLS), 0)
    lane = lax.broadcasted_iota(jnp.int32, (8, QROWS), 1)
    lane_group = jnp.full((8, QROWS), -1, jnp.int32)
    for s in range(4):
        for j in range(4):
            n = s * 4 + j
            rows = aligned(q_first[n])
            live = row < q_live[n]
            for a in range(2):
                qbuf[a, rows, :] = jnp.where(live, qd[s][j, a], qbuf[a, rows, :])
            here = (lane >= q_first[n]) & (lane < q_first[n] + q_live[n])
            lane_group = jnp.where(here, q_group[n], lane_group)
    qgrp[...] = lane_group


def load_keys(kv, kbuf, kgrp, k_group, k_live, k_first):
    kbuf[...] = jnp.zeros_like(kbuf)
    kgrp[...] = jnp.full_like(kgrp, FAR)
    row = lax.broadcasted_iota(jnp.int32, (PART, COLS), 0)
    row_lanes = lax.broadcasted_iota(jnp.int32, (PART, HD), 0)
    for j in range(4):
        for s in range(4):
            rows = aligned(k_first[j][s])
            live = row < k_live[j][s]
            for a in range(2):
                kbuf[a, rows, :] = jnp.where(live, kv[s][j, a], kbuf[a, rows, :])
            kgrp[rows, :] = jnp.where(row_lanes < k_live[j][s], k_group[j], kgrp[rows, :])


def stats_kernel(o, table, *refs):
    q_group, q_live, q_first = read_queries(table)
    k_group, k_live, k_first, blocks = read_keys(table, o)
    if o == 0:
        qbuf, qgrp, kbuf, kgrp, stats = refs[6:11]
        load_queries(pieces(*refs[0:3]), qbuf, qgrp, q_group, q_live, q_first)
    else:
        qbuf, qgrp, before = refs[0:3]
        kbuf, kgrp, stats = refs[6:9]
    load_keys(pieces(*refs[3:6]), kbuf, kgrp, k_group, k_live, k_first)
    stats[...] = jnp.zeros_like(stats)
    def chunk(n, _):
        rows = pl.ds(pl.multiple_of(n * QCHUNK, QCHUNK), QCHUNK)

        def step(keys, carry):
            group = kgrp[keys, :]
            ok = jnp.concatenate([group] * (QCHUNK // HD), axis=1) <= qgrp[0:1, rows]
            out = []
            for h in range(HEADS):
                cols = slice(h * HD, (h + 1) * HD)
                top, total, weighted = carry[h]
                scores = dot(kbuf[0, keys, cols], qbuf[0, rows, cols], NT)
                dprobs = dot(kbuf[1, keys, cols], qbuf[1, rows, cols], NT)
                scores = jnp.where(ok, scores * (SCALE * LOG2E), NEG)
                new_top = jnp.maximum(top, jnp.max(scores, axis=0, keepdims=True))
                weights = jnp.exp2(scores - new_top)
                factor = jnp.exp2(top - new_top)
                total = total * factor + jnp.sum(weights, axis=0, keepdims=True)
                weighted = weighted * factor + jnp.sum(weights * dprobs, axis=0, keepdims=True)
                out.append((new_top, total, weighted))
            return tuple(out)

        if o == 0:
            start = (
                jnp.full((1, QCHUNK), LOW, jnp.float32),
                jnp.zeros((1, QCHUNK), jnp.float32),
                jnp.zeros((1, QCHUNK), jnp.float32),
            )
            start = (start,) * HEADS
        else:
            start = tuple(
                tuple(before[3 * k + h : 3 * k + h + 1, rows] for k in range(3)) for h in range(HEADS)
            )
        final = visit(pick(blocks, n), step, start)
        for h in range(HEADS):
            for k in range(3):
                stats[3 * k + h : 3 * k + h + 1, rows] = final[h][k]
        return 0

    lax.fori_loop(0, QROWS // QCHUNK, chunk, 0)


def combine(parts, levels):
    sts = [st[...] for st in parts]
    top = functools.reduce(jnp.maximum, [st[0:3, :] for st in sts])
    factors = [jnp.exp2(st[0:3, :] - top) for st in sts]
    total = sum(f * st[3:6, :] for f, st in zip(factors, sts))
    weighted = sum(f * st[6:9, :] for f, st in zip(factors, sts))
    some = total > 0.0
    safe = jnp.where(some, total, 1.0)
    levels[0:3, :] = jnp.where(some, top + jnp.log2(safe), 0.0)
    levels[3:6, :] = weighted / safe
    levels[6:8, :] = jnp.zeros_like(levels[6:8, :])


def grad_kernel(o, table, qbuf, qgrp, kbuf, kgrp, *refs):
    q_group, q_live, q_first = read_queries(table)
    k_group, k_live, k_first, blocks = read_keys(table, o)
    if o == 1:
        dkv, dqt, levels, dks, dvs = refs[4:9]
        combine(refs[0:4], levels)
        dqt[...] = jnp.zeros_like(dqt)
    else:
        before, levels, dkv, dq, dqt, dks, dvs, dqs = refs
        dqt[...] = before[...]
    dks[...] = jnp.zeros_like(dks)
    dvs[...] = jnp.zeros_like(dvs)

    def chunk(n, _):
        rows = pl.ds(pl.multiple_of(n * QCHUNK, QCHUNK), QCHUNK)

        def step(keys, _):
            group = kgrp[keys, :]
            ok = jnp.concatenate([group] * (QCHUNK // HD), axis=1) <= qgrp[0:1, rows]
            products = []
            for h in range(HEADS):
                cols = slice(h * HD, (h + 1) * HD)
                scores = dot(kbuf[0, keys, cols], qbuf[0, rows, cols], NT)
                products.append((scores, dot(kbuf[1, keys, cols], qbuf[1, rows, cols], NT)))
            weights = []
            for h in range(HEADS):
                scores, dprobs = products[h]
                scores = jnp.where(ok, scores * (SCALE * LOG2E), NEG)
                probs = jnp.exp2(scores - levels[h : h + 1, rows])
                dscores = probs * (dprobs - levels[3 + h : 4 + h, rows])
                weights.append((probs.astype(jnp.bfloat16), dscores.astype(jnp.bfloat16)))
            for h in range(HEADS):
                cols = slice(h * HD, (h + 1) * HD)
                probs, dscores = weights[h]
                dvs[keys, cols] += dot(probs, qbuf[1, rows, cols], NN)
                dks[keys, cols] += dot(dscores, qbuf[0, rows, cols], NN)
                dqt[h, :, rows] += dot(kbuf[0, keys, cols], dscores, TN)
            return 0

        visit(pick(blocks, n), step, 0)
        return 0

    lax.fori_loop(0, QROWS // QCHUNK, chunk, 0)
    row = lax.broadcasted_iota(jnp.int32, (PART, COLS), 0)
    for j in range(4):
        for s in range(4):
            rows = aligned(k_first[j][s])
            live = row < k_live[j][s]
            dkv[s, j, 0] = jnp.where(live, dks[rows, :] * SCALE, 0.0).astype(jnp.bfloat16)
            dkv[s, j, 1] = jnp.where(live, dvs[rows, :], 0.0).astype(jnp.bfloat16)
    if o == 0:
        for h in range(HEADS):
            dqs[:, h * HD : (h + 1) * HD] = (dqt[h] * SCALE).T
        for s in range(4):
            for j in range(4):
                n = s * 4 + j
                rows = aligned(q_first[n])
                dq[s, j] = jnp.where(row < q_live[n], dqs[rows, :], 0.0).astype(jnp.bfloat16)


SMEM = pl.BlockSpec(memory_space=pltpu.SMEM)
VMEM = pl.BlockSpec(memory_space=pltpu.VMEM)
PARAMS = pltpu.CompilerParams(vmem_limit_bytes=24 * 1024 * 1024)
LARGE = pltpu.CompilerParams(vmem_limit_bytes=60 * 1024 * 1024)
SMALL = pltpu.CompilerParams(vmem_limit_bytes=6 * 1024 * 1024)


def run(kernel, name, out_shape, tables, arrays, scratch=()):
    return pl.pallas_call(
        kernel,
        out_shape=out_shape,
        in_specs=[SMEM] * len(tables) + [VMEM] * len(arrays),
        out_specs=(VMEM,) * len(out_shape),
        scratch_shapes=list(scratch),
        compiler_params=PARAMS,
        cost_estimate=pl.CostEstimate(flops=3 * 10**9, bytes_accessed=6 * 10**6, transcendentals=2 * 10**6),
        name=name,
    )(*tables, *arrays)


def local(query, keys, values, dout, slot_group, valid):
    c = lax.axis_index("head") % NC
    bf16, f32 = jnp.bfloat16, jnp.float32

    keep, give = pl.pallas_call(
        pack_kernel,
        out_shape=(jax.ShapeDtypeStruct((4, 4, SUB, COLS), bf16),) * 2,
        in_specs=[pl.BlockSpec(memory_space=pltpu.HBM)] * 4,
        out_specs=(VMEM,) * 2,
        scratch_shapes=[pltpu.VMEM((4, SUB, NZ * COLS), bf16), pltpu.SemaphoreType.DMA((4,))],
        compiler_params=LARGE,
        name="pack",
    )(query, dout, keys, values)
    take = swap_core(give)
    both = jnp.where(c == 0, jnp.concatenate([keep, take], axis=2), jnp.concatenate([take, keep], axis=2))
    i32 = jnp.int32
    slot_group, valid, both = lax.optimization_barrier((slot_group, valid, both))
    table = pl.pallas_call(
        table_kernel,
        out_shape=jax.ShapeDtypeStruct((128,), i32),
        in_specs=[SMEM] * 2,
        out_specs=SMEM,
        compiler_params=SMALL,
        cost_estimate=pl.CostEstimate(flops=2 * 10**9, bytes_accessed=10**6, transcendentals=0),
        name="table",
    )(slot_group, valid)
    got = {j: send(both[j], lambda y, z, x, c: (y, z + c + 2 * j, x, c)) for j in (2, 1, 3, 0)}
    own_qd = jnp.stack([got[j][0:2] for j in range(4)])
    own_kv = jnp.stack([got[j][2:4] for j in range(4)])

    kv_first, qd_first, table = lax.optimization_barrier((first_x(own_kv), first_y(own_qd), table))
    tables = (table,)
    kv_rest = second_x(jnp.stack([own_kv, kv_first]))
    qd_rest = second_y(jnp.stack([own_qd, qd_first]))

    kbuf_type = jax.ShapeDtypeStruct((2, KROWS, COLS), bf16)
    kgrp_type = jax.ShapeDtypeStruct((KROWS, HD), i32)
    stats_type = jax.ShapeDtypeStruct((16, QROWS), f32)
    qbuf, qgrp, kbuf, kgrp, part = run(
        functools.partial(stats_kernel, 0),
        "stats_own",
        (jax.ShapeDtypeStruct((2, QROWS, COLS), bf16), jax.ShapeDtypeStruct((8, QROWS), i32))
        + (kbuf_type, kgrp_type, stats_type),
        tables,
        (own_qd, qd_first, qd_rest, own_kv, kv_first, kv_rest),
    )
    kbuf_other, kgrp_other, stats = run(
        functools.partial(stats_kernel, 1),
        "stats_other",
        (kbuf_type, kgrp_type, stats_type),
        tables,
        (qbuf, qgrp, part, swap_core(own_kv), swap_core(kv_first), swap_core(kv_rest)),
    )

    all_stats = [stats] + [send(stats, lambda y, z, x, c: (y + n, z, x, c)) for n in (1, 2, 3)]

    dkv_type = jax.ShapeDtypeStruct((4, 4, 2, PART, COLS), bf16)
    scratch = [
        pltpu.VMEM((HEADS, HD, QROWS), f32),
        pltpu.VMEM((KROWS, COLS), f32),
        pltpu.VMEM((KROWS, COLS), f32),
    ]
    dkv_other, dqt, levels = run(
        functools.partial(grad_kernel, 1),
        "grads_other",
        (
            dkv_type,
            jax.ShapeDtypeStruct((HEADS, HD, QROWS), f32),
            jax.ShapeDtypeStruct((8, QROWS), f32),
        ),
        tables,
        (qbuf, qgrp, kbuf_other, kgrp_other, *all_stats),
        scratch[1:],
    )
    swapped = swap_core(dkv_other)
    dkv_own, dq = run(
        functools.partial(grad_kernel, 0),
        "grads_own",
        (dkv_type, jax.ShapeDtypeStruct((4, 4, PART, COLS), bf16)),
        tables,
        (qbuf, qgrp, kbuf, kgrp, dqt, levels),
        scratch + [pltpu.VMEM((QROWS, COLS), f32)],
    )

    dkv_sum = dkv_own.astype(f32) + swapped.astype(f32)
    dkv_half, dq_half = lax.optimization_barrier((second_x(dkv_sum[2:4].astype(bf16)), second_y(dq[2:4])))
    dkv_sum = dkv_sum[0:2] + dkv_half.astype(f32)
    dq_sum = dq[0:2].astype(f32) + dq_half.astype(f32)
    dkv_last, dq_last = lax.optimization_barrier(
        (first_x(dkv_sum[1].astype(bf16)), first_y(dq_sum[1].astype(bf16)))
    )
    dkv_sum = (dkv_sum[0] + dkv_last.astype(f32)).astype(bf16)
    dq_sum = (dq_sum[0] + dq_last.astype(f32)).astype(bf16)

    back = {}
    for j in (2, 1, 3, 0):
        block = jnp.concatenate([dq_sum[j][None], dkv_sum[j]], axis=0)
        back[j] = send(block, lambda y, z, x, c: (y, z - c - 2 * j, x, c))
    back = [back[j] for j in range(4)]
    first = jnp.stack([b[:, :SUB] for b in back])
    second = jnp.stack([b[:, SUB:] for b in back])
    theirs = swap_core(jnp.where(c == 0, second, first))
    return pl.pallas_call(
        unpack_kernel,
        out_shape=(jax.ShapeDtypeStruct((SUB, NZ * COLS), bf16),) * 3,
        in_specs=[VMEM] * 2,
        out_specs=(VMEM,) * 3,
        compiler_params=SMALL,
        name="unpack",
    )(jnp.where(c == 0, first, second), theirs)


def solution(mesh):
    spec = P(("tm", "head"), None)
    return jax.shard_map(
        local,
        mesh=mesh,
        in_specs=(spec, spec, spec, spec, P(), P()),
        out_specs=(spec, spec, spec),
        check_vma=False,
    )
```
